32 devices in a mesh: groups: 2 (over y), ctx: 8 (over z, x), tp: 2 (over core).
Axes of the slice: x: 2, y: 2, z: 4, core: 2. Of those that a mesh axis runs over, the one named last changes fastest.
Arguments:
- tokens: bfloat16 [4096, 2688], P(('groups', 'ctx', 'tp')), parts along dimension 0, may hold values from -6 to 6
- output_gradient: bfloat16 [4096, 2688], P(('groups', 'ctx', 'tp')), parts along dimension 0, may hold values from -6 to 6
- document_index: int32 [4096], P(('groups', 'ctx')), parts along dimension 0, may hold values from 0 to 3, never falling along the last dimension, each value on 1 to 1024 neighbouring positions
- real_token_count: int32 [16], P(('groups', 'ctx')), parts along dimension 0, may hold values from 64 to 256, as said below
- input_norm_gain: float32 [2688], replicated, may hold values from 0.1 to 1.9
- query_norm_gain: float32 [128], replicated, may hold values from 0.1 to 1.9
- key_norm_gain: float32 [128], replicated, may hold values from 0.1 to 1.9
- output_norm_gain: float32 [2688], replicated, may hold values from 0.1 to 1.9
- query_projection: bfloat16 [2688, 512], P(None, 'tp'), may hold values from -0.125 to 0.125
- key_projection: bfloat16 [2688, 256], P(None, 'tp'), may hold values from -0.125 to 0.125
- value_projection: bfloat16 [2688, 256], P(None, 'tp'), may hold values from -0.125 to 0.125
- output_projection: bfloat16 [512, 2688], P('tp'), may hold values from -0.25 to 0.25
- adapter_down_maps: bfloat16 [2688, 48], replicated, may hold values from -0.125 to 0.125
- adapter_query_up: bfloat16 [16, 512], P(None, 'tp'), may hold values from -0.375 to 0.375
- adapter_key_up: bfloat16 [16, 256], P(None, 'tp'), may hold values from -0.375 to 0.375
- adapter_value_up: bfloat16 [16, 256], P(None, 'tp'), may hold values from -0.375 to 0.375
- adapter_output_down: bfloat16 [512, 16], P('tp'), may hold values from -0.25 to 0.25
- adapter_output_up: bfloat16 [16, 2688], replicated, may hold values from -0.375 to 0.375
Outputs:
- layer_out: bfloat16 [4096, 2688], P(('groups', 'ctx', 'tp')), parts along dimension 0
- grad_in: bfloat16 [4096, 2688], P(('groups', 'ctx', 'tp')), parts along dimension 0
- grad_down: float32 [5376, 48], P(('groups', 'tp')), parts along dimension 0
- query_up_gradient: float32 [32, 512], P('groups', 'tp'), parts along dimension 0
- key_up_gradient: float32 [32, 256], P('groups', 'tp'), parts along dimension 0
- value_up_gradient: float32 [32, 256], P('groups', 'tp'), parts along dimension 0
- grad_down_out: float32 [1024, 16], P(('groups', 'tp')), parts along dimension 0
- output_up_gradient: float32 [32, 2688], P('groups', 'tp'), parts along dimension 0
The draws below stay inside these ranges and needn't reach their ends.
There are 2 independent parts, one for each index of `groups`. The reference program is written for one: setup_inputs(seed, part) draws one part's arguments, and reference() takes and returns one part's arrays. A program takes and returns all parts, laid end to end along the dimension named above; an argument that names none is the same for every part. Nothing has to cross between parts.
Inputs may be any that keep to these rules, and one draw needn't show every extreme that they name: `document_index`: document numbers never fall along the tokens; a document has 1 to 1024 tokens and one has exactly that many. `real_token_count`: the real tokens of a block come first and the rest is padding; some block is full and some holds 64 real tokens.
All inputs are finite; a program needn't handle non-finite values.
Results may differ from the reference program's by a relative error of at most 0.034.
Values may be sent and summed in bfloat16 or wider, within the bound.
A program may use at most 64 MiB of HBM per device.

```python
import math
import jax
import jax.numpy as jnp
import numpy as np
from jax import lax

MODEL_DIMENSION = 2688
HEAD_DIMENSION = 128
HEADS_DEV = 2
ADAPTER_RANK = 16
WINDOW = 1024
T_CTX = 256
QUERY_HEAD_COUNT = 4
KEY_VALUE_HEADS = 2
TOKENS = 2048
N_CTX = 8
N_TP = 2


def draw_real_token_count(key, part):
    first_key, second_key, third_key = jax.random.split(key, 3)
    counts_drawn = jax.random.randint(first_key, (N_CTX,), T_CTX // 4, T_CTX + 1)
    full_at = jax.random.randint(second_key, (), 0, N_CTX)
    short_at = (full_at + 1 + jax.random.randint(third_key, (), 0, N_CTX - 1)) % N_CTX
    places = jnp.arange(N_CTX)
    counts_drawn = jnp.where(places == full_at, T_CTX, counts_drawn)
    counts_drawn = jnp.where(places == short_at, T_CTX // 4, counts_drawn)
    return counts_drawn.astype(jnp.int32)


def block_scale(key, dims, cuts, low, top_value):
    loudness = 1.0
    for position, blocks in cuts:
        heights = jax.random.uniform(jax.random.fold_in(jax.random.fold_in(key, 6), position), (blocks,), jnp.float32, low / len(cuts), top_value / len(cuts))
        loudness = loudness * jnp.repeat(jnp.exp(heights), dims[position] // blocks).reshape((-1,) + (1,) * (len(dims) - 1 - position))
    return loudness


def length_profile(number_of, total, limit, slope):
    portions = [(1 << 20) // math.isqrt(standing ** slope) + 1 for standing in range(2, number_of + 1)]
    rest, given = total - limit - (number_of - 1), [1] * (number_of - 1)
    while rest > 0:
        free = [i for i in range(number_of - 1) if given[i] < limit]
        mass, budget = sum([portions[i] for i in free]), rest
        for i in free:
            more = min(limit - given[i], max(1, budget * portions[i] // mass), rest)
            given[i] = given[i] + more
            rest = rest - more
    return np.array([limit] + given)


def uneven(stream_key, amount, total, limit, skew):
    if amount == 2:
        one = jax.random.randint(stream_key, (), max(1, total - limit), min(limit, total - 1) + 1)
        return jnp.stack([one, total - one])
    sizes = jnp.asarray(length_profile(amount, total, limit, skew), jnp.int32)
    twos = (amount - 1) // 2
    giver, receiver = sizes[1:1 + 2 * twos:2], sizes[2:2 + 2 * twos:2]
    margin = jnp.minimum(giver - 1, limit - receiver)
    shifted = jax.random.randint(jax.random.fold_in(stream_key, 1), (twos,), 0, 1 << 20) % (margin + 1)
    sizes = sizes.at[1:1 + 2 * twos:2].set(giver - shifted).at[2:2 + 2 * twos:2].set(receiver + shifted)
    return sizes[jax.random.permutation(jax.random.fold_in(stream_key, 2), amount)]


def gaussian(stream_key, shape, spread, most, cuts=(), held_as=jnp.bfloat16):
    entries = jax.random.normal(stream_key, shape, jnp.float32) * spread
    if len(cuts) > 0:
        entries = block_scale(stream_key, shape, cuts, -0.22, 0.18) * entries
    return jnp.clip(entries, min=-most, max=most).astype(held_as)


def setup_inputs(seed: int = 0, part: int = 0) -> dict:
    key_list = jax.random.split(jax.random.key(seed), 19)
    own_keys = jax.random.split(jax.random.fold_in(key_list[18], part), 19)
    tokens = gaussian(own_keys[0], (TOKENS, MODEL_DIMENSION), 1.0, 6.0, ((0, 16),))
    output_gradient = gaussian(own_keys[1], (TOKENS, MODEL_DIMENSION), 1.0, 6.0, ((0, 16),))
    document_index = jnp.searchsorted(jnp.cumsum(uneven(own_keys[2], max(2, N_CTX // 2), TOKENS, TOKENS // 2, 2)), jnp.arange(TOKENS), side="right").astype(jnp.int32)
    real_token_count = draw_real_token_count(jax.random.fold_in(jax.random.fold_in(key_list[18], part), 71), part)
    input_norm_gain = jnp.clip(1.0 + 0.18 * jax.random.normal(key_list[4], (MODEL_DIMENSION,), jnp.float32), 0.1, 1.9)
    query_norm_gain = jnp.clip(1.0 + 0.18 * jax.random.normal(key_list[5], (HEAD_DIMENSION,), jnp.float32), 0.1, 1.9)
    key_norm_gain = jnp.clip(1.0 + 0.18 * jax.random.normal(key_list[6], (HEAD_DIMENSION,), jnp.float32), 0.1, 1.9)
    output_norm_gain = jnp.clip(1.0 + 0.18 * jax.random.normal(key_list[7], (MODEL_DIMENSION,), jnp.float32), 0.1, 1.9)
    query_projection = gaussian(key_list[8], (MODEL_DIMENSION, QUERY_HEAD_COUNT * HEAD_DIMENSION), MODEL_DIMENSION ** -0.5, 0.125, ((1, 2),))
    key_projection = gaussian(key_list[9], (MODEL_DIMENSION, KEY_VALUE_HEADS * HEAD_DIMENSION), MODEL_DIMENSION ** -0.5, 0.125, ((1, 2),))
    value_projection = gaussian(key_list[10], (MODEL_DIMENSION, KEY_VALUE_HEADS * HEAD_DIMENSION), MODEL_DIMENSION ** -0.5, 0.125, ((1, 2),))
    output_projection = gaussian(key_list[11], (QUERY_HEAD_COUNT * HEAD_DIMENSION, MODEL_DIMENSION), (QUERY_HEAD_COUNT * HEAD_DIMENSION) ** -0.5, 0.25, ((0, 2),))
    adapter_down_maps = gaussian(key_list[12], (MODEL_DIMENSION, 3 * ADAPTER_RANK), MODEL_DIMENSION ** -0.5, 0.125)
    adapter_query_up = gaussian(key_list[13], (ADAPTER_RANK, QUERY_HEAD_COUNT * HEAD_DIMENSION), (16 * ADAPTER_RANK) ** -0.5, 0.375, ((1, 2),))
    adapter_key_up = gaussian(key_list[14], (ADAPTER_RANK, KEY_VALUE_HEADS * HEAD_DIMENSION), (16 * ADAPTER_RANK) ** -0.5, 0.375, ((1, 2),))
    adapter_value_up = gaussian(key_list[15], (ADAPTER_RANK, KEY_VALUE_HEADS * HEAD_DIMENSION), (16 * ADAPTER_RANK) ** -0.5, 0.375, ((1, 2),))
    adapter_output_down = gaussian(key_list[16], (QUERY_HEAD_COUNT * HEAD_DIMENSION, ADAPTER_RANK), (QUERY_HEAD_COUNT * HEAD_DIMENSION) ** -0.5, 0.25, ((0, 2),))
    adapter_output_up = gaussian(key_list[17], (ADAPTER_RANK, MODEL_DIMENSION), (16 * ADAPTER_RANK) ** -0.5, 0.375)
    return dict(tokens=tokens, output_gradient=output_gradient, document_index=document_index, real_token_count=real_token_count, input_norm_gain=input_norm_gain, query_norm_gain=query_norm_gain, key_norm_gain=key_norm_gain, output_norm_gain=output_norm_gain, query_projection=query_projection, key_projection=key_projection, value_projection=value_projection, output_projection=output_projection, adapter_down_maps=adapter_down_maps, adapter_query_up=adapter_query_up, adapter_key_up=adapter_key_up, adapter_value_up=adapter_value_up, adapter_output_down=adapter_output_down, adapter_output_up=adapter_output_up)


epsilon = 1e-06
adapter_scale = 2.0
score_scale = 168.0 ** (-0.5)

def norm_rows(source, gain_vec):
    inverse = lax.rsqrt(lax.optimization_barrier(jnp.mean(source * source, axis=-1, keepdims=True)) + epsilon)
    return source * inverse * gain_vec

def norm_back(source, gain_vec, incoming):
    inverse = lax.rsqrt(lax.optimization_barrier(jnp.mean(source * source, axis=-1, keepdims=True)) + epsilon)
    scaled = source * inverse
    upward = incoming * gain_vec
    return inverse * (upward - scaled * lax.optimization_barrier(jnp.mean(upward * scaled, axis=-1, keepdims=True)))

def matrix_product(first_op, second_op):
    return jnp.dot(first_op, second_op, preferred_element_type=jnp.float32)

def rounded(source):
    return lax.optimization_barrier(source.astype(jnp.bfloat16)).astype(jnp.float32)

def window_mask(query_segs, key_codes):
    query_count = query_segs.shape[0]
    key_total = key_codes.shape[0]
    distance = (key_total - query_count + jnp.arange(query_count))[:, None] - jnp.arange(key_total)[None, :]
    same_doc = key_codes[None, :] == query_segs[:, None] + 1
    return (distance == 0) | (distance > 0) & (distance < WINDOW) & same_doc

def divide_groups(source, head_groups, per_width):
    return jnp.swapaxes(source.reshape(source.shape[0], head_groups, per_width), 0, 1)

def reference(tokens, output_gradient, document_index, real_token_count, input_norm_gain, query_norm_gain, key_norm_gain, output_norm_gain, query_projection, key_projection, value_projection, output_projection, adapter_down_maps, adapter_query_up, adapter_key_up, adapter_value_up, adapter_output_down, adapter_output_up):
    head_groups = N_TP
    head_total = HEADS_DEV * head_groups
    heads_per_group = HEADS_DEV * HEAD_DIMENSION
    tok_float = tokens.astype(jnp.float32)
    is_valid = (jnp.arange(T_CTX, dtype=jnp.int32)[None, :] < real_token_count[:, None]).reshape(TOKENS)
    real_token_fraction = is_valid.astype(jnp.float32)
    codes_all = jnp.where(is_valid, document_index + 1, 0).astype(jnp.int32)
    normalized_input = norm_rows(tok_float, input_norm_gain).astype(jnp.bfloat16)
    middle_list = matrix_product(normalized_input, adapter_down_maps).astype(jnp.bfloat16)
    middle_query = middle_list[:, :ADAPTER_RANK]
    middle_key = middle_list[:, ADAPTER_RANK:2 * ADAPTER_RANK]
    middle_value = middle_list[:, 2 * ADAPTER_RANK:]
    query_before_norm = matrix_product(normalized_input, query_projection) + adapter_scale * matrix_product(middle_query, adapter_query_up)
    key_before_norm = matrix_product(normalized_input, key_projection) + adapter_scale * matrix_product(middle_key, adapter_key_up)
    value_before_norm = matrix_product(normalized_input, value_projection) + adapter_scale * matrix_product(middle_value, adapter_value_up)
    query_heads = query_before_norm.reshape(TOKENS, head_groups, HEADS_DEV, HEAD_DIMENSION)
    query_normed = norm_rows(query_heads, query_norm_gain).astype(jnp.bfloat16)
    key_heads = key_before_norm.reshape(TOKENS, head_groups, HEAD_DIMENSION)
    key_normed = norm_rows(key_heads, key_norm_gain).astype(jnp.bfloat16)
    value_cast = value_before_norm.reshape(TOKENS, head_groups, HEAD_DIMENSION).astype(jnp.bfloat16)
    key_padded = jnp.concatenate([jnp.zeros((WINDOW, head_groups, HEAD_DIMENSION), jnp.bfloat16), key_normed], 0)
    value_padded = jnp.concatenate([jnp.zeros((WINDOW, head_groups, HEAD_DIMENSION), jnp.bfloat16), value_cast], 0)
    code_padded = jnp.concatenate([jnp.zeros((WINDOW,), jnp.int32), codes_all], 0)
    key_span = WINDOW + T_CTX

    def block_probs(block_start):
        queries = lax.dynamic_slice_in_dim(query_normed, block_start, T_CTX, 0).astype(jnp.float32)
        keys_here = lax.dynamic_slice_in_dim(key_padded, block_start, key_span, 0).astype(jnp.float32)
        values_here = lax.dynamic_slice_in_dim(value_padded, block_start, key_span, 0).astype(jnp.float32)
        codes_here = lax.dynamic_slice_in_dim(code_padded, block_start, key_span, 0)
        segs_here = lax.dynamic_slice_in_dim(document_index, block_start, T_CTX, 0)
        allowed = window_mask(segs_here, codes_here)
        scores = jnp.einsum('tgjd,sgd->gjts', queries, keys_here) * score_scale
        weights = jnp.where(allowed, jnp.exp(scores), 0.0)
        attn_probs = weights / lax.optimization_barrier(jnp.sum(weights, axis=-1, keepdims=True))
        return (queries, keys_here, values_here, attn_probs)

    def attend(block_index):
        block_start = (block_index * T_CTX).astype(jnp.int32)
        queries, keys_here, values_here, attn_probs = block_probs(block_start)
        result = jnp.einsum('gjts,sgd->tgjd', rounded(attn_probs), values_here)
        mask_rows = lax.dynamic_slice_in_dim(real_token_fraction, block_start, T_CTX, 0)
        return (result * mask_rows[:, None, None, None]).astype(jnp.bfloat16)
    blocks = jnp.arange(N_CTX, dtype=jnp.int32)
    attention_result = lax.map(attend, blocks).reshape(TOKENS, head_total * HEAD_DIMENSION)
    att_groups = divide_groups(attention_result, head_groups, heads_per_group)
    out_groups = output_projection.reshape(head_groups, heads_per_group, MODEL_DIMENSION)
    down_weight_groups = adapter_output_down.reshape(head_groups, heads_per_group, ADAPTER_RANK)

    def add_group(carried, pieces):
        total_out, total_mid = carried
        att_piece, out_piece, down_piece = pieces
        total_out = total_out + rounded(matrix_product(att_piece, out_piece))
        total_mid = total_mid + rounded(matrix_product(att_piece, down_piece))
        return ((total_out, total_mid), None)
    start_sums = (jnp.zeros((TOKENS, MODEL_DIMENSION), jnp.float32), jnp.zeros((TOKENS, ADAPTER_RANK), jnp.float32))
    (output_total, mid_sum), ignored = lax.scan(add_group, start_sums, (att_groups, out_groups, down_weight_groups))
    middle_output = mid_sum.astype(jnp.bfloat16)
    apply_prenorm = output_total + adapter_scale * matrix_product(middle_output, adapter_output_up)
    layer_out = norm_rows(apply_prenorm, output_norm_gain).astype(jnp.bfloat16)
    prenorm_gradient = norm_back(apply_prenorm, output_norm_gain, output_gradient.astype(jnp.float32)).astype(jnp.bfloat16)
    middle_output_gradient = (adapter_scale * matrix_product(prenorm_gradient, adapter_output_up.T)).astype(jnp.bfloat16)
    output_up_gradient = adapter_scale * matrix_product(middle_output.T, prenorm_gradient)
    attention_gradient = (matrix_product(prenorm_gradient, output_projection.T) + matrix_product(middle_output_gradient, adapter_output_down.T)) * real_token_fraction[:, None]
    attention_gradient = attention_gradient.astype(jnp.bfloat16)
    grad_down_out = matrix_product(attention_result.T, middle_output_gradient)
    grad_att_heads = attention_gradient.reshape(TOKENS, head_groups, HEADS_DEV, HEAD_DIMENSION)

    def back_block(carried, block_index):
        key_acc, value_acc = carried
        block_start = (block_index * T_CTX).astype(jnp.int32)
        queries, keys_here, values_here, attn_probs = block_probs(block_start)
        grad_heads = lax.dynamic_slice_in_dim(grad_att_heads, block_start, T_CTX, 0).astype(jnp.float32)
        grad_probs = jnp.einsum('tgjd,sgd->gjts', grad_heads, values_here)
        inner_sum = lax.optimization_barrier(jnp.sum(attn_probs * grad_probs, axis=-1, keepdims=True))
        grad_scores = rounded(attn_probs * (grad_probs - inner_sum) * score_scale)
        grad_query = jnp.einsum('gjts,sgd->tgjd', grad_scores, keys_here)
        grad_keys = jnp.einsum('gjts,tgjd->sgd', grad_scores, queries)
        grad_values = jnp.einsum('gjts,tgjd->sgd', rounded(attn_probs), grad_heads)
        key_acc = lax.dynamic_update_slice_in_dim(key_acc, lax.dynamic_slice_in_dim(key_acc, block_start, key_span, 0) + grad_keys, block_start, 0)
        value_acc = lax.dynamic_update_slice_in_dim(value_acc, lax.dynamic_slice_in_dim(value_acc, block_start, key_span, 0) + grad_values, block_start, 0)
        return ((key_acc, value_acc), grad_query)
    zeros_pad = jnp.zeros((WINDOW + TOKENS, head_groups, HEAD_DIMENSION), jnp.float32)
    (key_acc, value_acc), grad_query_blocks = lax.scan(back_block, (zeros_pad, zeros_pad), blocks)
    grad_query_all = grad_query_blocks.reshape(TOKENS, head_groups, HEADS_DEV, HEAD_DIMENSION)
    query_prenorm_gradient = norm_back(query_heads, query_norm_gain, grad_query_all).reshape(TOKENS, head_total * HEAD_DIMENSION).astype(jnp.bfloat16)
    key_prenorm_gradient = norm_back(key_heads, key_norm_gain, key_acc[WINDOW:]).reshape(TOKENS, head_groups * HEAD_DIMENSION).astype(jnp.bfloat16)
    value_prenorm_gradient = value_acc[WINDOW:].reshape(TOKENS, head_groups * HEAD_DIMENSION).astype(jnp.bfloat16)
    query_up_gradient = adapter_scale * matrix_product(middle_query.T, query_prenorm_gradient)
    key_up_gradient = adapter_scale * matrix_product(middle_key.T, key_prenorm_gradient)
    value_up_gradient = adapter_scale * matrix_product(middle_value.T, value_prenorm_gradient)
    collected_pieces = (divide_groups(query_prenorm_gradient, head_groups, heads_per_group), divide_groups(key_prenorm_gradient, head_groups, HEAD_DIMENSION), divide_groups(value_prenorm_gradient, head_groups, HEAD_DIMENSION), jnp.swapaxes(query_projection.reshape(MODEL_DIMENSION, head_groups, heads_per_group), 0, 1), jnp.swapaxes(key_projection.reshape(MODEL_DIMENSION, head_groups, HEAD_DIMENSION), 0, 1), jnp.swapaxes(value_projection.reshape(MODEL_DIMENSION, head_groups, HEAD_DIMENSION), 0, 1), jnp.swapaxes(adapter_query_up.reshape(ADAPTER_RANK, head_groups, heads_per_group), 0, 1), jnp.swapaxes(adapter_key_up.reshape(ADAPTER_RANK, head_groups, HEAD_DIMENSION), 0, 1), jnp.swapaxes(adapter_value_up.reshape(ADAPTER_RANK, head_groups, HEAD_DIMENSION), 0, 1))

    def back_group(carried, pieces):
        total_grad, total_down = carried
        query_gradient, key_gradient, value_gradient, query_weight_total, key_weight_total, value_weight_total, query_up_product, key_up_product, value_up_product = pieces
        middle_gradient_list = jnp.concatenate([adapter_scale * matrix_product(query_gradient, query_up_product.T), adapter_scale * matrix_product(key_gradient, key_up_product.T), adapter_scale * matrix_product(value_gradient, value_up_product.T)], 1).astype(jnp.bfloat16)
        group_contribution = matrix_product(query_gradient, query_weight_total.T) + matrix_product(key_gradient, key_weight_total.T) + matrix_product(value_gradient, value_weight_total.T) + matrix_product(middle_gradient_list, adapter_down_maps.T)
        total_grad = total_grad + rounded(group_contribution)
        total_down = total_down + matrix_product(normalized_input.T, middle_gradient_list)
        return ((total_grad, total_down), None)
    start_back = (jnp.zeros((TOKENS, MODEL_DIMENSION), jnp.float32), jnp.zeros((MODEL_DIMENSION, 3 * ADAPTER_RANK), jnp.float32))
    (grad_normed, grad_down), ignored = lax.scan(back_group, start_back, collected_pieces)
    grad_in = norm_back(tok_float, input_norm_gain, grad_normed).astype(jnp.bfloat16)
    return (layer_out, grad_in, grad_down, query_up_gradient, key_up_gradient, value_up_gradient, grad_down_out, output_up_gradient)
```

```python
import jax
import jax.numpy as jnp
from jax import lax
from jax.experimental import pallas as pl
from jax.experimental.pallas import tpu as pltpu
from jax.sharding import PartitionSpec as P

WINDOW = 1024
LANES = 128
NORM_ROWS = 16

epsilon = 1e-06
adapter_scale = 2.0
score_scale = 168.0 ** (-0.5)

bf16 = jnp.bfloat16
f32 = jnp.float32


def norm_rows(source, gain_vec):
    inverse = lax.rsqrt(jnp.mean(source * source, axis=-1, keepdims=True) + epsilon)
    return source * inverse * gain_vec


def norm_back(source, gain_vec, incoming):
    inverse = lax.rsqrt(jnp.mean(source * source, axis=-1, keepdims=True) + epsilon)
    scaled = source * inverse
    upward = incoming * gain_vec
    return inverse * (upward - scaled * jnp.mean(upward * scaled, axis=-1, keepdims=True))


def matrix_product(first_op, second_op):
    return jnp.dot(first_op, second_op, preferred_element_type=f32)


def multiply_by_transpose(first_op, second_op):
    return lax.dot_general(
        first_op, second_op, (((1,), (1,)), ((), ())), preferred_element_type=f32
    )


def window_of(model_width, tp_size):
    slice_width = model_width // tp_size
    if slice_width % LANES == 0:
        return slice_width, slice_width
    width = min(-(-(slice_width + LANES - 1) // LANES) * LANES, model_width)
    if tp_size == 2:
        width = -(-slice_width // LANES) * LANES
    return slice_width, width


def window_start(tp_index, slice_width, width, model_width):
    return jnp.minimum(tp_index * slice_width // LANES * LANES, model_width - width)


def layer_kernel(
    shapes,
    tokens,
    output_gradient,
    documents,
    token_count,
    input_gain,
    query_gain,
    key_gain,
    output_gain,
    query_w,
    key_w,
    value_w,
    output_w,
    down_w,
    query_up,
    key_up,
    value_up,
    out_down,
    out_up,
    layer_out,
    grad_in,
    sums_out,
    normed,
    codes,
    pairs,
    weights,
    attended,
    out_send,
    out_recv,
    mid_send,
    mid_recv,
    pre_norm,
    grad_full,
    small_full,
    pair_grads,
    pair_recv,
    query_pre,
    key_pre,
    pre_grads,
    mid_pad,
    mid_grads,
    mid_grads_recv,
    normed_send,
    normed_recv,
    grad_normed,
    sums_send,
    sums_recv,
    sums_all,
    gather_sems,
    code_sems,
    pair_sems,
    out_sems,
    mid_sems,
    grad_sems,
    small_sems,
    back_sems,
    mid_grad_sems,
    normed_sems,
    sum_sems,
    total_sems,
):
    ctx_size, tp_size, reach, hops = shapes
    rows, model = tokens.shape
    block = documents.shape[1]
    head = key_w.shape[1]
    heads = query_w.shape[1] // head
    rank = key_up.shape[0]
    ctx = lax.axis_index("ctx")
    tp = lax.axis_index("tp")

    def tp_at(step):
        return lax.rem(tp + step, tp_size)

    def ctx_at(step):
        return lax.rem(ctx + step, ctx_size)

    def remote(source, target, sems, slot, where):
        return pltpu.make_async_remote_copy(
            src_ref=source,
            dst_ref=target,
            send_sem=sems.at[0, slot],
            recv_sem=sems.at[1, slot],
            device_id=where,
            device_id_type=pl.DeviceIdType.MESH,
        )

    def rows_of(index):
        return pl.ds(pl.multiple_of(index * rows, rows), rows)

    mine = rows_of(tp)

    barrier = pltpu.get_barrier_semaphore()
    for step in range(1, tp_size):
        pl.semaphore_signal(
            barrier, inc=1, device_id={"tp": tp_at(step)}, device_id_type=pl.DeviceIdType.MESH
        )
    for step in range(1, ctx_size):
        pl.semaphore_signal(
            barrier, inc=1, device_id={"ctx": ctx_at(step)}, device_id_type=pl.DeviceIdType.MESH
        )

    def norm_chunk(index, carry):
        at = pl.ds(pl.multiple_of(index * NORM_ROWS, NORM_ROWS), NORM_ROWS)
        to = pl.ds(pl.multiple_of(tp * rows + index * NORM_ROWS, NORM_ROWS), NORM_ROWS)
        normed[to, :] = norm_rows(tokens[at, :].astype(f32), input_gain[...]).astype(bf16)
        return carry

    lax.fori_loop(0, rows // NORM_ROWS, norm_chunk, 0)

    lane_pos = lax.broadcasted_iota(jnp.int32, (1, block), 1)
    valid_lane = (lane_pos < token_count[0]).astype(f32)
    valid_sub = (
        lax.broadcasted_iota(jnp.int32, (block, 1), 0) < token_count[0]
    ).astype(f32)
    own_codes = jnp.where(lane_pos < token_count[0], documents[...] + 1, 0)
    codes[0] = jnp.broadcast_to(own_codes, codes.shape[1:])
    for hop in range(1, hops + 1):

        @pl.when(ctx < hop)
        def _(hop=hop):
            codes[hop] = jnp.zeros(codes.shape[1:], codes.dtype)
            pairs[hop] = jnp.zeros(pairs.shape[1:], pairs.dtype)

        @pl.when(ctx + hop >= ctx_size)
        def _(hop=hop):
            pair_recv[hop - 1] = jnp.zeros(pair_recv.shape[1:], pair_recv.dtype)

    pl.semaphore_wait(barrier, tp_size - 1 + ctx_size - 1)

    gathers = []
    for step in range(1, tp_size):
        copy = remote(
            normed.at[mine], normed.at[mine], gather_sems, step - 1, {"tp": tp_at(step)}
        )
        copy.start()
        gathers.append(copy)

    def code_copy(hop):
        return remote(codes.at[0], codes.at[hop], code_sems, hop - 1, {"ctx": ctx_at(hop)})

    def pair_copy(hop):
        return remote(pairs.at[0], pairs.at[hop], pair_sems, hop - 1, {"ctx": ctx_at(hop)})

    def back_copy(hop):
        return remote(
            pair_grads.at[hop - 1],
            pair_recv.at[hop - 1],
            back_sems,
            hop - 1,
            {"ctx": ctx_at(ctx_size - hop)},
        )

    for hop in range(1, hops + 1):

        @pl.when(ctx + hop < ctx_size)
        def _(hop=hop):
            code_copy(hop).start()

    for copy in gathers:
        copy.wait()

    inputs = normed[...]
    middles = matrix_product(inputs, down_w[...]).astype(bf16)
    mid_pad[...] = jnp.zeros(mid_pad.shape, f32)
    mid_pad[:, : 3 * rank] = middles.astype(f32)

    def projected(weight, up, place):
        return matrix_product(inputs, weight[...]) + adapter_scale * matrix_product(
            middles[:, place * rank : (place + 1) * rank], up[...]
        )

    key_pre[...] = projected(key_w, key_up, 1)
    pairs[0, :, :head] = norm_rows(key_pre[...], key_gain[...]).astype(bf16)
    pairs[0, :, head:] = projected(value_w, value_up, 2).astype(bf16)
    for hop in range(1, hops + 1):

        @pl.when(ctx + hop < ctx_size)
        def _(hop=hop):
            pair_copy(hop).start()

    query_pre[...] = projected(query_w, query_up, 0)
    query_list = [
        norm_rows(query_pre[:, h * head : (h + 1) * head], query_gain[...]) for h in range(heads)
    ]
    query_rows = jnp.concatenate(query_list, axis=0).astype(bf16)
    query_cols = jnp.concatenate([q.T for q in query_list], axis=1).astype(bf16)

    sub = lax.broadcasted_iota(jnp.int32, (block, block), 0)
    lane = lax.broadcasted_iota(jnp.int32, (block, block), 1)
    wanted = (documents[...] + 1).astype(f32)
    totals = jnp.zeros((1, heads * block), f32)
    outputs = jnp.zeros((head, heads * block), f32)
    for hop in range(hops + 1):
        if hop > 0:

            @pl.when(ctx >= hop)
            def _(hop=hop):
                code_copy(hop).wait_recv()
                pair_copy(hop).wait_recv()

        code_row = codes[hop][0:1, :].astype(f32)
        code_col = jnp.sum(jnp.where(sub == lane, code_row, 0.0), axis=1, keepdims=True)
        allowed = code_col == wanted
        if hop == 0:
            allowed = (sub == lane) | ((sub < lane) & allowed)
        if hop == reach:
            allowed = (sub > lane) & allowed
        allowed = allowed.astype(f32)
        allowed = jnp.concatenate([allowed] * heads, axis=1)
        scores = matrix_product(pairs[hop, :, :head], query_cols) * score_scale
        exps = jnp.where(allowed > 0.0, jnp.exp(scores), 0.0)
        totals = totals + jnp.sum(exps, axis=0, keepdims=True)
        exps = exps.astype(bf16)
        weights[hop] = exps
        values_cols = pairs[hop, :, head:].astype(f32).T.astype(bf16)
        outputs = outputs + matrix_product(values_cols, exps)
    inverse_totals = 1.0 / totals
    outputs = outputs * inverse_totals
    for h in range(heads):
        piece = outputs[:, h * block : (h + 1) * block] * valid_lane
        attended[:, h * head : (h + 1) * head] = piece.T.astype(bf16)

    mid_send[...] = jnp.zeros(mid_send.shape, bf16)
    out_copies = []
    for step in range(1, tp_size):
        theirs = attended[rows_of(tp_at(step)), :]
        mid_send[step - 1, :, :rank] = matrix_product(theirs, out_down[...]).astype(bf16)
        out_send[step - 1] = matrix_product(theirs, output_w[...]).astype(bf16)
        for source, target, sems in (
            (mid_send, mid_recv, mid_sems),
            (out_send, out_recv, out_sems),
        ):
            copy = remote(
                source.at[step - 1], target.at[step - 1], sems, step - 1, {"tp": tp_at(step)}
            )
            copy.start()
            out_copies.append(copy)
    own_rows = attended[mine, :]
    mid_sum = matrix_product(own_rows, out_down[...]).astype(bf16).astype(f32)
    pre_norm[...] = matrix_product(own_rows, output_w[...])
    for copy in out_copies:
        copy.wait()
    for step in range(1, tp_size):
        mid_sum = mid_sum + mid_recv[step - 1, :, :rank].astype(f32)
    mid_out = mid_sum.astype(bf16)
    pre_norm[...] += adapter_scale * matrix_product(mid_out, out_up[...])

    def out_chunk(index, carry):
        at = pl.ds(pl.multiple_of(index * NORM_ROWS, NORM_ROWS), NORM_ROWS)
        to = pl.ds(pl.multiple_of(tp * rows + index * NORM_ROWS, NORM_ROWS), NORM_ROWS)
        held = pre_norm[at, :]
        for step in range(1, tp_size):
            held = held + out_recv[step - 1, at, :].astype(f32)
        layer_out[at, :] = norm_rows(held, output_gain[...]).astype(bf16)
        grad_full[to, :] = norm_back(
            held, output_gain[...], output_gradient[at, :].astype(f32)
        ).astype(bf16)
        return carry

    lax.fori_loop(0, rows // NORM_ROWS, out_chunk, 0)

    grad_copies = []
    for step in range(1, tp_size):
        copy = remote(
            grad_full.at[mine], grad_full.at[mine], grad_sems, step - 1, {"tp": tp_at(step)}
        )
        copy.start()
        grad_copies.append(copy)
    grad_mid_out = adapter_scale * multiply_by_transpose(grad_full[mine, :], out_up[...])
    small_full[mine, :] = jnp.zeros((rows, 2 * LANES), bf16)
    small_full[mine, :rank] = grad_mid_out.astype(bf16)
    small_full[mine, LANES : LANES + rank] = mid_out
    for step in range(1, tp_size):
        copy = remote(
            small_full.at[mine], small_full.at[mine], small_sems, step - 1, {"tp": tp_at(step)}
        )
        copy.start()
        grad_copies.append(copy)
    for copy in grad_copies:
        copy.wait()

    grad_att = (
        multiply_by_transpose(grad_full[...], output_w[...])
        + multiply_by_transpose(small_full[:, :rank], out_down[...])
    ) * valid_sub
    grad_cols = jnp.concatenate(
        [grad_att[:, h * head : (h + 1) * head].T for h in range(heads)], axis=1
    ).astype(bf16)
    grad_float = grad_cols.astype(f32)
    inner = jnp.sum(grad_float * outputs, axis=0, keepdims=True)
    grad_rows = (grad_float * inverse_totals).T.astype(bf16)
    row_scale = inverse_totals * score_scale

    query_back = jnp.zeros((head, heads * block), f32)
    own_keys = own_values = None
    for hop in range(hops, -1, -1):
        keys = pairs[hop, :, :head]
        exps = weights[hop]
        probs_back = matrix_product(pairs[hop, :, head:], grad_cols)
        scores_back = (exps.astype(f32) * ((probs_back - inner) * row_scale)).astype(bf16)
        keys_back = matrix_product(scores_back, query_rows)
        values_back = matrix_product(exps, grad_rows)
        query_back = query_back + matrix_product(keys.astype(f32).T.astype(bf16), scores_back)
        if hop > 0:
            pair_grads[hop - 1, :, :head] = keys_back.astype(bf16)
            pair_grads[hop - 1, :, head:] = values_back.astype(bf16)

            @pl.when(ctx >= hop)
            def _(hop=hop):
                back_copy(hop).start()

        else:
            own_keys, own_values = keys_back, values_back
    query_width = heads * head
    for h in range(heads):
        at = slice(h * head, (h + 1) * head)
        pre_grads[:, at] = norm_back(
            query_pre[:, at], query_gain[...], query_back[:, h * block : (h + 1) * block].T
        ).astype(bf16)
    for hop in range(1, hops + 1):

        @pl.when(ctx + hop < ctx_size)
        def _(hop=hop):
            back_copy(hop).wait_recv()

        own_keys = own_keys + pair_recv[hop - 1, :, :head].astype(f32)
        own_values = own_values + pair_recv[hop - 1, :, head:].astype(f32)
    key_at = slice(query_width, query_width + head)
    value_at = slice(query_width + head, query_width + 2 * head)
    pre_grads[:, key_at] = norm_back(key_pre[...], key_gain[...], own_keys).astype(bf16)
    pre_grads[:, value_at] = own_values.astype(bf16)

    mid_grads[...] = jnp.zeros(mid_grads.shape, bf16)
    for place, (at, up) in enumerate(
        ((slice(0, query_width), query_up), (key_at, key_up), (value_at, value_up))
    ):
        mid_grads[:, place * rank : (place + 1) * rank] = (
            adapter_scale * multiply_by_transpose(pre_grads[:, at], up[...])
        ).astype(bf16)
    last_copies = []
    for step in range(1, tp_size):
        copy = remote(
            mid_grads, mid_grads_recv.at[step - 1], mid_grad_sems, step - 1, {"tp": tp_at(step)}
        )
        copy.start()
        last_copies.append(copy)

    def input_part(which):
        grads = pre_grads[which, :]
        return (
            multiply_by_transpose(grads[:, :query_width], query_w[...])
            + multiply_by_transpose(grads[:, key_at], key_w[...])
            + multiply_by_transpose(grads[:, value_at], value_w[...])
            + multiply_by_transpose(mid_grads[which, : 3 * rank], down_w[...])
        )

    normed_copies = []
    for step in range(1, tp_size):
        normed_send[step - 1] = input_part(rows_of(tp_at(step))).astype(bf16)
        copy = remote(
            normed_send.at[step - 1],
            normed_recv.at[step - 1],
            normed_sems,
            step - 1,
            {"tp": tp_at(step)},
        )
        copy.start()
        normed_copies.append(copy)

    slice_width, width = window_of(model, tp_size)
    start = window_start(tp, slice_width, width, model)
    window = pl.ds(pl.multiple_of(start, LANES), width)
    for copy in last_copies:
        copy.wait()
    mid_total = mid_grads[...].astype(f32)
    for step in range(1, tp_size):
        mid_total = mid_total + mid_grads_recv[step - 1].astype(f32)
    mid_total = mid_total.T[: 3 * rank].astype(bf16)
    middle_cols = mid_pad[...].T[: 3 * rank].astype(bf16)
    small_cols = small_full[...].astype(f32).T
    grad_mid_cols = small_cols[:rank].astype(bf16)
    mid_out_cols = small_cols[LANES : LANES + rank].astype(bf16)
    main_terms = jnp.concatenate(
        [
            matrix_product(mid_total, normed[:, window]),
            adapter_scale * matrix_product(mid_out_cols, grad_full[:, window]),
        ],
        axis=0,
    ).astype(bf16)
    up_terms = [
        adapter_scale * matrix_product(middle_cols[:rank], pre_grads[:, :query_width]),
        adapter_scale
        * jnp.concatenate(
            [
                matrix_product(middle_cols[rank : 2 * rank], pre_grads[:, key_at]),
                matrix_product(middle_cols[2 * rank :], pre_grads[:, value_at]),
            ],
            axis=1,
        ),
        matrix_product(grad_mid_cols, attended[...]),
        jnp.zeros((rank, query_width), f32),
    ]
    piece_width = sums_send.shape[2]
    padding = piece_width * ctx_size - width - query_width
    pieces = [main_terms, jnp.concatenate(up_terms, axis=0).astype(bf16)]
    if padding > 0:
        pieces.append(jnp.zeros((4 * rank, padding), bf16))
    every_term = jnp.concatenate(pieces, axis=1)
    for index in range(ctx_size):
        sums_send[index] = every_term[:, index * piece_width : (index + 1) * piece_width]
    sum_copies = []
    for step in range(1, ctx_size):
        copy = remote(
            sums_send.at[ctx_at(step)],
            sums_recv.at[step - 1],
            sum_sems,
            step - 1,
            {"ctx": ctx_at(step)},
        )
        copy.start()
        sum_copies.append(copy)

    grad_normed[...] = input_part(mine)
    for copy in sum_copies:
        copy.wait()
    total = sums_send[ctx].astype(f32)
    for step in range(1, ctx_size):
        total = total + sums_recv[step - 1].astype(f32)
    sums_all[ctx] = total.astype(bf16)
    total_copies = []
    for step in range(1, ctx_size):
        copy = remote(
            sums_all.at[ctx], sums_all.at[ctx], total_sems, step - 1, {"ctx": ctx_at(step)}
        )
        copy.start()
        total_copies.append(copy)

    for copy in normed_copies:
        copy.wait()

    def in_chunk(index, carry):
        at = pl.ds(pl.multiple_of(index * NORM_ROWS, NORM_ROWS), NORM_ROWS)
        incoming = grad_normed[at, :]
        for step in range(1, tp_size):
            incoming = incoming + normed_recv[step - 1, at, :].astype(f32)
        grad_in[at, :] = norm_back(
            tokens[at, :].astype(f32), input_gain[...], incoming
        ).astype(bf16)
        return carry

    lax.fori_loop(0, rows // NORM_ROWS, in_chunk, 0)

    for copy in total_copies:
        copy.wait()
    for index in range(ctx_size):
        sums_out[:, index * piece_width : (index + 1) * piece_width] = sums_all[index].astype(f32)

    for hop in range(1, hops + 1):

        @pl.when(ctx + hop < ctx_size)
        def _(hop=hop):
            code_copy(hop).wait_send()
            pair_copy(hop).wait_send()

        @pl.when(ctx >= hop)
        def _(hop=hop):
            back_copy(hop).wait_send()


def on_device(
    tokens,
    output_gradient,
    document_index,
    real_token_count,
    input_norm_gain,
    query_norm_gain,
    key_norm_gain,
    output_norm_gain,
    query_projection,
    key_projection,
    value_projection,
    output_projection,
    adapter_down_maps,
    adapter_query_up,
    adapter_key_up,
    adapter_value_up,
    adapter_output_down,
    adapter_output_up,
):
    rows, model = tokens.shape
    block = document_index.shape[0]
    head = key_projection.shape[1]
    query_width = query_projection.shape[1]
    rank = adapter_key_up.shape[0]
    ctx_size = lax.axis_size("ctx")
    tp_size = lax.axis_size("tp")
    tp_index = lax.axis_index("tp")
    reach = WINDOW // block
    hops = min(reach, ctx_size - 1)
    peers = max(tp_size - 1, 1)
    slice_width, width = window_of(model, tp_size)
    piece_width = -(-(width + query_width) // (LANES * ctx_size)) * LANES

    def kernel(*refs):
        layer_kernel((ctx_size, tp_size, reach, hops), *refs)

    whole = pl.BlockSpec(memory_space=pltpu.VMEM)
    in_specs = [whole] * 18
    in_specs[3] = pl.BlockSpec(memory_space=pltpu.SMEM)
    layer_out, grad_in, sums = pl.pallas_call(
        kernel,
        out_shape=(
            jax.ShapeDtypeStruct((rows, model), bf16),
            jax.ShapeDtypeStruct((rows, model), bf16),
            jax.ShapeDtypeStruct((4 * rank, piece_width * ctx_size), f32),
        ),
        in_specs=in_specs,
        out_specs=(whole, whole, whole),
        scratch_shapes=[
            pltpu.VMEM((block, model), bf16),
            pltpu.VMEM((hops + 1, 8, block), jnp.int32),
            pltpu.VMEM((hops + 1, block, 2 * head), bf16),
            pltpu.VMEM((hops + 1, block, query_width // head * block), bf16),
            pltpu.VMEM((block, query_width), bf16),
            pltpu.VMEM((peers, rows, model), bf16),
            pltpu.VMEM((peers, rows, model), bf16),
            pltpu.VMEM((peers, rows, LANES), bf16),
            pltpu.VMEM((peers, rows, LANES), bf16),
            pltpu.VMEM((rows, model), f32),
            pltpu.VMEM((block, model), bf16),
            pltpu.VMEM((block, 2 * LANES), bf16),
            pltpu.VMEM((hops, block, 2 * head), bf16),
            pltpu.VMEM((hops, block, 2 * head), bf16),
            pltpu.VMEM((block, query_width), f32),
            pltpu.VMEM((block, head), f32),
            pltpu.VMEM((block, query_width + 2 * head), bf16),
            pltpu.VMEM((block, LANES), f32),
            pltpu.VMEM((block, LANES), bf16),
            pltpu.VMEM((peers, block, LANES), bf16),
            pltpu.VMEM((peers, rows, model), bf16),
            pltpu.VMEM((peers, rows, model), bf16),
            pltpu.VMEM((rows, model), f32),
            pltpu.VMEM((ctx_size, 4 * rank, piece_width), bf16),
            pltpu.VMEM((ctx_size - 1, 4 * rank, piece_width), bf16),
            pltpu.VMEM((ctx_size, 4 * rank, piece_width), bf16),
            pltpu.SemaphoreType.DMA((2, peers)),
            pltpu.SemaphoreType.DMA((2, hops)),
            pltpu.SemaphoreType.DMA((2, hops)),
            pltpu.SemaphoreType.DMA((2, peers)),
            pltpu.SemaphoreType.DMA((2, peers)),
            pltpu.SemaphoreType.DMA((2, peers)),
            pltpu.SemaphoreType.DMA((2, peers)),
            pltpu.SemaphoreType.DMA((2, hops)),
            pltpu.SemaphoreType.DMA((2, peers)),
            pltpu.SemaphoreType.DMA((2, peers)),
            pltpu.SemaphoreType.DMA((2, ctx_size - 1)),
            pltpu.SemaphoreType.DMA((2, ctx_size - 1)),
        ],
        compiler_params=pltpu.CompilerParams(
            collective_id=0, has_side_effects=True, vmem_limit_bytes=56 * 1024 * 1024
        ),
    )(
        tokens,
        output_gradient,
        document_index.reshape(1, block),
        real_token_count,
        input_norm_gain.reshape(1, model),
        query_norm_gain.reshape(1, head),
        key_norm_gain.reshape(1, head),
        output_norm_gain.reshape(1, model),
        query_projection,
        key_projection,
        value_projection,
        output_projection,
        adapter_down_maps,
        adapter_query_up,
        adapter_key_up,
        adapter_value_up,
        adapter_output_down,
        adapter_output_up,
    )
    offset = tp_index * slice_width - window_start(tp_index, slice_width, width, model)
    share = lax.dynamic_slice_in_dim(sums[:, :width], offset, slice_width, 1)
    ups = sums[:, width : width + query_width]
    return (
        layer_out,
        grad_in,
        share[: 3 * rank].T,
        ups[:rank],
        ups[rank : 2 * rank, :head],
        ups[rank : 2 * rank, head : 2 * head],
        ups[2 * rank : 3 * rank].T,
        share[3 * rank :],
    )


def solution(mesh):
    in_specs = (
        P(("groups", "ctx", "tp"), None),
        P(("groups", "ctx", "tp"), None),
        P(("groups", "ctx")),
        P(("groups", "ctx")),
        P(),
        P(),
        P(),
        P(),
        P(None, "tp"),
        P(None, "tp"),
        P(None, "tp"),
        P("tp", None),
        P(),
        P(None, "tp"),
        P(None, "tp"),
        P(None, "tp"),
        P("tp", None),
        P(),
    )
    out_specs = (
        P(("groups", "ctx", "tp"), None),
        P(("groups", "ctx", "tp"), None),
        P(("groups", "tp"), None),
        P("groups", "tp"),
        P("groups", "tp"),
        P("groups", "tp"),
        P(("groups", "tp"), None),
        P("groups", "tp"),
    )
    return jax.shard_map(
        on_device, mesh=mesh, in_specs=in_specs, out_specs=out_specs, check_vma=False
    )
```

```python
import jax
import jax.numpy as jnp
from jax import lax
from jax.experimental import pallas as pl
from jax.experimental.pallas import tpu as pltpu
from jax.sharding import PartitionSpec as P

WINDOW = 1024
LANES = 128
NORM_ROWS = 16

epsilon = 1e-06
adapter_scale = 2.0
score_scale = 168.0 ** (-0.5)

bf16 = jnp.bfloat16
f32 = jnp.float32


def norm_rows(source, gain_vec):
    inverse = lax.rsqrt(jnp.mean(source * source, axis=-1, keepdims=True) + epsilon)
    return source * inverse * gain_vec


def norm_back(source, gain_vec, incoming):
    inverse = lax.rsqrt(jnp.mean(source * source, axis=-1, keepdims=True) + epsilon)
    scaled = source * inverse
    upward = incoming * gain_vec
    return inverse * (upward - scaled * jnp.mean(upward * scaled, axis=-1, keepdims=True))


def matrix_product(first_op, second_op):
    return jnp.dot(first_op, second_op, preferred_element_type=f32)


def multiply_by_transpose(first_op, second_op):
    return lax.dot_general(
        first_op, second_op, (((1,), (1,)), ((), ())), preferred_element_type=f32
    )


def window_of(model_width, tp_size):
    slice_width = model_width // tp_size
    if slice_width % LANES == 0:
        return slice_width, slice_width
    width = min(-(-(slice_width + LANES - 1) // LANES) * LANES, model_width)
    if tp_size == 2:
        width = -(-slice_width // LANES) * LANES
    return slice_width, width


def window_start(tp_index, slice_width, width, model_width):
    return jnp.minimum(tp_index * slice_width // LANES * LANES, model_width - width)


def layer_kernel(
    shapes,
    tokens,
    output_gradient,
    documents,
    token_count,
    input_gain_vec,
    query_gain,
    key_gain,
    output_gain_vec,
    query_w,
    key_w,
    value_w,
    output_w,
    down_w,
    query_up,
    key_up,
    value_up,
    out_down,
    out_up,
    layer_out,
    grad_in,
    down_out_rows,
    query_up_out,
    key_up_out,
    value_up_out,
    out_down_out,
    out_up_out,
    input_gain,
    output_gain,
    normed,
    codes,
    pairs,
    weights,
    attended,
    out_send,
    out_recv,
    mid_send,
    mid_recv,
    pre_norm,
    grad_full,
    small_full,
    pair_grads,
    pair_recv,
    query_pre,
    key_pre,
    pre_grads,
    mid_pad,
    mid_grads,
    mid_grads_recv,
    normed_send,
    normed_recv,
    grad_normed,
    sums_send,
    sums_recv,
    sums_all,
    gather_sems,
    code_sems,
    pair_sems,
    out_sems,
    mid_sems,
    grad_sems,
    small_sems,
    back_sems,
    mid_grad_sems,
    normed_sems,
    sum_sems,
    total_sems,
):
    ctx_size, tp_size, reach, hops = shapes
    rows, model = tokens.shape
    block = documents.shape[1]
    head = key_w.shape[1]
    heads = query_w.shape[1] // head
    rank = key_up.shape[0]
    ctx = lax.axis_index("ctx")
    tp = lax.axis_index("tp")

    def tp_at(step):
        return lax.rem(tp + step, tp_size)

    def ctx_at(step):
        return lax.rem(ctx + step, ctx_size)

    def remote(source, target, sems, slot, where):
        return pltpu.make_async_remote_copy(
            src_ref=source,
            dst_ref=target,
            send_sem=sems.at[0, slot],
            recv_sem=sems.at[1, slot],
            device_id=where,
            device_id_type=pl.DeviceIdType.MESH,
        )

    def rows_of(index):
        return pl.ds(pl.multiple_of(index * rows, rows), rows)

    mine = rows_of(tp)

    barrier = pltpu.get_barrier_semaphore()
    for step in range(1, tp_size):
        pl.semaphore_signal(
            barrier, inc=1, device_id={"tp": tp_at(step)}, device_id_type=pl.DeviceIdType.MESH
        )
    for step in range(1, ctx_size):
        pl.semaphore_signal(
            barrier, inc=1, device_id={"ctx": ctx_at(step)}, device_id_type=pl.DeviceIdType.MESH
        )

    input_gain[...] = input_gain_vec[...].reshape(1, model)
    output_gain[...] = output_gain_vec[...].reshape(1, model)

    def norm_chunk(index, carry):
        at = pl.ds(pl.multiple_of(index * NORM_ROWS, NORM_ROWS), NORM_ROWS)
        to = pl.ds(pl.multiple_of(tp * rows + index * NORM_ROWS, NORM_ROWS), NORM_ROWS)
        normed[to, :] = norm_rows(tokens[at, :].astype(f32), input_gain[...]).astype(bf16)
        return carry

    lax.fori_loop(0, rows // NORM_ROWS, norm_chunk, 0)

    lane_pos = lax.broadcasted_iota(jnp.int32, (1, block), 1)
    valid_lane = (lane_pos < token_count[0]).astype(f32)
    valid_sub = (
        lax.broadcasted_iota(jnp.int32, (block, 1), 0) < token_count[0]
    ).astype(f32)
    own_codes = jnp.where(lane_pos < token_count[0], documents[...] + 1, 0)
    codes[0] = jnp.broadcast_to(own_codes, codes.shape[1:])
    for hop in range(1, hops + 1):

        @pl.when(ctx < hop)
        def _(hop=hop):
            codes[hop] = jnp.zeros(codes.shape[1:], codes.dtype)
            pairs[hop] = jnp.zeros(pairs.shape[1:], pairs.dtype)

    odd = lax.rem(ctx, 2) == 1
    even = jnp.logical_not(odd)
    has_up = ctx + 2 < ctx_size
    partner = {"ctx": ctx + 1 - 2 * lax.rem(ctx, 2)}
    above = {"ctx": ctx_at(2)}
    below = {"ctx": ctx_at(ctx_size - 2)}
    arrives = (
        (even & (ctx >= 2)) | (odd & (ctx >= 5)),
        has_up & (ctx >= 2),
        even | (ctx >= 3),
        has_up,
    )
    sends = (
        (even & (ctx >= 4)) | (odd & (ctx >= 3)),
        ctx >= 4,
        odd | (ctx >= 2),
        ctx >= 2,
    )
    for place in range(4):

        @pl.when(jnp.logical_not(arrives[place]))
        def _(place=place):
            pair_recv[place] = jnp.zeros(pair_recv.shape[1:], pair_recv.dtype)

    pl.semaphore_wait(barrier, tp_size - 1 + ctx_size - 1)

    gathers = []
    for step in range(1, tp_size):
        copy = remote(
            normed.at[mine], normed.at[mine], gather_sems, step - 1, {"tp": tp_at(step)}
        )
        copy.start()
        gathers.append(copy)

    def code_copy(hop):
        return remote(codes.at[0], codes.at[hop], code_sems, hop - 1, {"ctx": ctx_at(hop)})

    def pair_copy(source, target, where):
        return remote(pairs.at[source], pairs.at[target], pair_sems, target - 1, where)

    def back_copy(hop, place, where):
        return remote(pair_grads.at[hop - 1], pair_recv.at[place], back_sems, place, where)

    pair_arrives = {1: odd | (ctx >= 2), 2: ctx >= 2, 3: ctx >= 3, 4: ctx >= 4}
    pair_arrives[3] = (odd & (ctx >= 3)) | (even & (ctx >= 4))

    for hop in range(1, hops + 1):

        @pl.when(ctx + hop < ctx_size)
        def _(hop=hop):
            code_copy(hop).start()

    for copy in gathers:
        copy.wait()

    inputs = normed[...]
    middles = multiply_by_transpose(inputs, down_w[...]).astype(bf16)
    mid_pad[...] = jnp.zeros(mid_pad.shape, f32)
    mid_pad[:, : 3 * rank] = middles.astype(f32)

    def projected(weight, up, place):
        return matrix_product(inputs, weight[...]) + adapter_scale * matrix_product(
            middles[:, place * rank : (place + 1) * rank], up[...]
        )

    key_pre[...] = projected(key_w, key_up, 1)
    pairs[0, :, :head] = norm_rows(key_pre[...], key_gain[...]).astype(bf16)
    pairs[0, :, head:] = projected(value_w, value_up, 2).astype(bf16)

    @pl.when(has_up)
    def _():
        pair_copy(0, 2, above).start()

    @pl.when(even)
    def _():
        pair_copy(0, 1, partner).start()

    query_pre[...] = projected(query_w, query_up, 0)
    query_list = [
        norm_rows(query_pre[:, h * head : (h + 1) * head], query_gain[...]) for h in range(heads)
    ]
    query_rows = jnp.concatenate(query_list, axis=0).astype(bf16)
    query_cols = jnp.concatenate([q.T for q in query_list], axis=1).astype(bf16)

    sub = lax.broadcasted_iota(jnp.int32, (block, block), 0)
    lane = lax.broadcasted_iota(jnp.int32, (block, block), 1)
    wanted = (documents[...] + 1).astype(f32)
    totals = jnp.zeros((1, heads * block), f32)
    outputs = jnp.zeros((head, heads * block), f32)
    for hop in range(1, hops + 1):

        @pl.when(ctx >= hop)
        def _(hop=hop):
            code_copy(hop).wait_recv()

    def receive_pair(hop):
        @pl.when(pair_arrives[hop])
        def _():
            pair_copy(0, hop, partner).wait_recv()

    receive_pair(2)

    @pl.when(has_up & (ctx >= 2))
    def _():
        pair_copy(2, 4, above).start()

    @pl.when(even & (ctx >= 2))
    def _():
        pair_copy(2, 3, partner).start()

    @pl.when(odd & (ctx >= 2))
    def _():
        pair_copy(2, 1, partner).start()

    for hop in (0, 2, 1, 4, 3):
        if hop == 1:
            receive_pair(1)
            receive_pair(4)

            @pl.when(odd & (ctx >= 4))
            def _():
                pair_copy(4, 3, partner).start()

        if hop == 3:
            receive_pair(3)
        code_row = codes[hop][0:1, :].astype(f32)
        code_col = jnp.sum(jnp.where(sub == lane, code_row, 0.0), axis=1, keepdims=True)
        allowed = code_col == wanted
        if hop == 0:
            allowed = (sub == lane) | ((sub < lane) & allowed)
        if hop == reach:
            allowed = (sub > lane) & allowed
        allowed = allowed.astype(f32)
        allowed = jnp.concatenate([allowed] * heads, axis=1)
        scores = matrix_product(pairs[hop, :, :head], query_cols) * score_scale
        exps = jnp.where(allowed > 0.0, jnp.exp(scores), 0.0)
        totals = totals + jnp.sum(exps, axis=0, keepdims=True)
        exps = exps.astype(bf16)
        weights[hop] = exps
        values_cols = pairs[hop, :, head:].astype(f32).T.astype(bf16)
        outputs = outputs + matrix_product(values_cols, exps)
    inverse_totals = 1.0 / totals
    outputs = outputs * inverse_totals
    for h in range(heads):
        piece = outputs[:, h * block : (h + 1) * block] * valid_lane
        attended[:, h * head : (h + 1) * head] = piece.T.astype(bf16)

    mid_send[...] = jnp.zeros(mid_send.shape, bf16)
    out_copies = []
    for step in range(1, tp_size):
        theirs = attended[rows_of(tp_at(step)), :]
        mid_send[step - 1, :, :rank] = multiply_by_transpose(theirs, out_down[...]).astype(bf16)
        out_send[step - 1] = matrix_product(theirs, output_w[...]).astype(bf16)
        for source, target, sems in (
            (mid_send, mid_recv, mid_sems),
            (out_send, out_recv, out_sems),
        ):
            copy = remote(
                source.at[step - 1], target.at[step - 1], sems, step - 1, {"tp": tp_at(step)}
            )
            copy.start()
            out_copies.append(copy)
    own_rows = attended[mine, :]
    mid_sum = multiply_by_transpose(own_rows, out_down[...]).astype(bf16).astype(f32)
    pre_norm[...] = matrix_product(own_rows, output_w[...])
    for copy in out_copies:
        copy.wait()
    for step in range(1, tp_size):
        mid_sum = mid_sum + mid_recv[step - 1, :, :rank].astype(f32)
    mid_out = mid_sum.astype(bf16)
    pre_norm[...] += adapter_scale * matrix_product(mid_out, out_up[...])

    def out_chunk(index, carry):
        at = pl.ds(pl.multiple_of(index * NORM_ROWS, NORM_ROWS), NORM_ROWS)
        to = pl.ds(pl.multiple_of(tp * rows + index * NORM_ROWS, NORM_ROWS), NORM_ROWS)
        held = pre_norm[at, :]
        for step in range(1, tp_size):
            held = held + out_recv[step - 1, at, :].astype(f32)
        layer_out[at, :] = norm_rows(held, output_gain[...]).astype(bf16)
        grad_full[to, :] = norm_back(
            held, output_gain[...], output_gradient[at, :].astype(f32)
        ).astype(bf16)
        return carry

    lax.fori_loop(0, rows // NORM_ROWS, out_chunk, 0)

    grad_copies = []
    for step in range(1, tp_size):
        copy = remote(
            grad_full.at[mine], grad_full.at[mine], grad_sems, step - 1, {"tp": tp_at(step)}
        )
        copy.start()
        grad_copies.append(copy)
    grad_mid_out = adapter_scale * multiply_by_transpose(grad_full[mine, :], out_up[...])
    small_full[mine, :] = jnp.zeros((rows, 2 * LANES), bf16)
    small_full[mine, :rank] = grad_mid_out.astype(bf16)
    small_full[mine, LANES : LANES + rank] = mid_out
    for step in range(1, tp_size):
        copy = remote(
            small_full.at[mine], small_full.at[mine], small_sems, step - 1, {"tp": tp_at(step)}
        )
        copy.start()
        grad_copies.append(copy)
    for copy in grad_copies:
        copy.wait()

    grad_att = (
        multiply_by_transpose(grad_full[...], output_w[...])
        + matrix_product(small_full[:, :rank], out_down[...])
    ) * valid_sub
    grad_cols = jnp.concatenate(
        [grad_att[:, h * head : (h + 1) * head].T for h in range(heads)], axis=1
    ).astype(bf16)
    grad_float = grad_cols.astype(f32)
    inner = jnp.sum(grad_float * outputs, axis=0, keepdims=True)
    grad_rows = (grad_float * inverse_totals).T.astype(bf16)
    row_scale = inverse_totals * score_scale

    query_back = jnp.zeros((head, heads * block), f32)
    odd_share = odd.astype(f32)
    even_share = 1.0 - odd_share

    def receive_back(place):
        @pl.when(arrives[place])
        def _():
            back_copy(1, place, partner).wait_recv()

    def send_back(hop, place, where, sends):
        @pl.when(sends)
        def _():
            back_copy(hop, place, where).start()

    for hop in (3, 4, 1, 2, 0):
        keys = pairs[hop, :, :head]
        exps = weights[hop]
        probs_back = matrix_product(pairs[hop, :, head:], grad_cols)
        scores_back = (exps.astype(f32) * ((probs_back - inner) * row_scale)).astype(bf16)
        keys_back = matrix_product(scores_back, query_rows)
        values_back = matrix_product(exps, grad_rows)
        query_back = query_back + matrix_product(keys.astype(f32).T.astype(bf16), scores_back)
        pair_back = jnp.concatenate([keys_back, values_back], axis=1)
        if hop == 3:
            pair_grads[2] = pair_back.astype(bf16)
            send_back(3, 0, partner, sends[0])
        if hop == 4:
            receive_back(0)
            pair_back = pair_back + odd_share * pair_recv[0].astype(f32)
            pair_grads[3] = pair_back.astype(bf16)
            send_back(4, 1, below, sends[1])
        if hop == 1:
            pair_grads[0] = pair_back.astype(bf16)
            send_back(1, 2, partner, sends[2])
        if hop == 2:
            receive_back(2)
            receive_back(1)
            pair_back = pair_back + even_share * pair_recv[0].astype(f32)
            pair_back = pair_back + odd_share * pair_recv[2].astype(f32)
            pair_back = pair_back + pair_recv[1].astype(f32)
            pair_grads[1] = pair_back.astype(bf16)
            send_back(2, 3, below, sends[3])
        if hop == 0:
            own_pair = pair_back + even_share * pair_recv[2].astype(f32)
    query_width = heads * head
    for h in range(heads):
        at = slice(h * head, (h + 1) * head)
        pre_grads[:, at] = norm_back(
            query_pre[:, at], query_gain[...], query_back[:, h * block : (h + 1) * block].T
        ).astype(bf16)
    receive_back(3)
    own_pair = own_pair + pair_recv[3].astype(f32)
    own_keys, own_values = own_pair[:, :head], own_pair[:, head:]
    key_at = slice(query_width, query_width + head)
    value_at = slice(query_width + head, query_width + 2 * head)
    pre_grads[:, key_at] = norm_back(key_pre[...], key_gain[...], own_keys).astype(bf16)
    pre_grads[:, value_at] = own_values.astype(bf16)

    mid_grads[...] = jnp.zeros(mid_grads.shape, bf16)
    for place, (at, up) in enumerate(
        ((slice(0, query_width), query_up), (key_at, key_up), (value_at, value_up))
    ):
        mid_grads[:, place * rank : (place + 1) * rank] = (
            adapter_scale * multiply_by_transpose(pre_grads[:, at], up[...])
        ).astype(bf16)
    last_copies = []
    for step in range(1, tp_size):
        copy = remote(
            mid_grads, mid_grads_recv.at[step - 1], mid_grad_sems, step - 1, {"tp": tp_at(step)}
        )
        copy.start()
        last_copies.append(copy)

    def input_part(which):
        grads = pre_grads[which, :]
        return (
            multiply_by_transpose(grads[:, :query_width], query_w[...])
            + multiply_by_transpose(grads[:, key_at], key_w[...])
            + multiply_by_transpose(grads[:, value_at], value_w[...])
            + matrix_product(mid_grads[which, : 3 * rank], down_w[...])
        )

    slice_width, width = window_of(model, tp_size)
    start = window_start(tp, slice_width, width, model)
    window = pl.ds(pl.multiple_of(start, LANES), width)
    for copy in last_copies:
        copy.wait()
    mid_total = mid_grads[...].astype(f32)
    for step in range(1, tp_size):
        mid_total = mid_total + mid_grads_recv[step - 1].astype(f32)
    mid_total = mid_total.T[: 3 * rank].astype(bf16)
    middle_cols = mid_pad[...].T[: 3 * rank].astype(bf16)
    small_cols = small_full[...].astype(f32).T
    grad_mid_cols = small_cols[:rank].astype(bf16)
    mid_out_cols = small_cols[LANES : LANES + rank].astype(bf16)
    main_terms = jnp.concatenate(
        [
            matrix_product(mid_total, normed[:, window]),
            adapter_scale * matrix_product(mid_out_cols, grad_full[:, window]),
        ],
        axis=0,
    ).astype(bf16)
    up_terms = [
        adapter_scale * matrix_product(middle_cols[:rank], pre_grads[:, :query_width]),
        adapter_scale
        * jnp.concatenate(
            [
                matrix_product(middle_cols[rank : 2 * rank], pre_grads[:, key_at]),
                matrix_product(middle_cols[2 * rank :], pre_grads[:, value_at]),
            ],
            axis=1,
        ),
        matrix_product(grad_mid_cols, attended[...]),
        jnp.zeros((rank, query_width), f32),
    ]
    piece_width = sums_send.shape[2]
    padding = piece_width * ctx_size - width - query_width
    pieces = [main_terms, jnp.concatenate(up_terms, axis=0).astype(bf16)]
    if padding > 0:
        pieces.append(jnp.zeros((4 * rank, padding), bf16))
    every_term = jnp.concatenate(pieces, axis=1)
    for index in range(ctx_size):
        sums_send[index] = every_term[:, index * piece_width : (index + 1) * piece_width]
    sum_copies = []
    for step in range(1, ctx_size):
        copy = remote(
            sums_send.at[ctx_at(step)],
            sums_recv.at[step - 1],
            sum_sems,
            step - 1,
            {"ctx": ctx_at(step)},
        )
        copy.start()
        sum_copies.append(copy)

    normed_copies = []
    for step in range(1, tp_size):
        normed_send[step - 1] = input_part(rows_of(tp_at(step))).astype(bf16)
        copy = remote(
            normed_send.at[step - 1],
            normed_recv.at[step - 1],
            normed_sems,
            step - 1,
            {"tp": tp_at(step)},
        )
        copy.start()
        normed_copies.append(copy)

    grad_normed[...] = input_part(mine)
    for copy in sum_copies:
        copy.wait()
    total = sums_send[ctx].astype(f32)
    for step in range(1, ctx_size):
        total = total + sums_recv[step - 1].astype(f32)
    sums_all[ctx] = total.astype(bf16)
    total_copies = []
    for step in range(1, ctx_size):
        copy = remote(
            sums_all.at[ctx], sums_all.at[ctx], total_sems, step - 1, {"ctx": ctx_at(step)}
        )
        copy.start()
        total_copies.append(copy)

    for copy in normed_copies:
        copy.wait()

    def in_chunk(index, carry):
        at = pl.ds(pl.multiple_of(index * NORM_ROWS, NORM_ROWS), NORM_ROWS)
        incoming = grad_normed[at, :]
        for step in range(1, tp_size):
            incoming = incoming + normed_recv[step - 1, at, :].astype(f32)
        grad_in[at, :] = norm_back(
            tokens[at, :].astype(f32), input_gain[...], incoming
        ).astype(bf16)
        return carry

    lax.fori_loop(0, rows // NORM_ROWS, in_chunk, 0)

    for copy in total_copies:
        copy.wait()
    sums = jnp.concatenate([sums_all[index].astype(f32) for index in range(ctx_size)], axis=1)
    offset = tp * slice_width - start
    share = pltpu.roll(sums[:, :width], lax.rem(width - offset, width), 1)[:, :slice_width]
    ups = sums[:, width : width + query_width]
    down_out_rows[...] = share[: 3 * rank]
    out_up_out[...] = share[3 * rank :]
    query_up_out[...] = ups[:rank]
    key_up_out[...] = ups[rank : 2 * rank, :head]
    value_up_out[...] = ups[rank : 2 * rank, head : 2 * head]
    out_down_out[...] = ups[2 * rank : 3 * rank]

    for hop in range(1, hops + 1):

        @pl.when(ctx + hop < ctx_size)
        def _(hop=hop):
            code_copy(hop).wait_send()

    for target, sent in (
        (1, even | (ctx >= 2)),
        (2, has_up),
        (3, (even & (ctx >= 2)) | (odd & (ctx >= 4))),
        (4, has_up & (ctx >= 2)),
    ):

        @pl.when(sent)
        def _(target=target):
            pair_copy(0, target, partner).wait_send()

    for place in range(4):

        @pl.when(sends[place])
        def _(place=place):
            back_copy(1, place, partner).wait_send()


def on_device(
    tokens,
    output_gradient,
    document_index,
    real_token_count,
    input_norm_gain,
    query_norm_gain,
    key_norm_gain,
    output_norm_gain,
    query_projection,
    key_projection,
    value_projection,
    output_projection,
    adapter_down_maps,
    adapter_query_up,
    adapter_key_up,
    adapter_value_up,
    adapter_output_down,
    adapter_output_up,
):
    rows, model = tokens.shape
    block = document_index.shape[0]
    head = key_projection.shape[1]
    query_width = query_projection.shape[1]
    rank = adapter_key_up.shape[0]
    ctx_size = lax.axis_size("ctx")
    tp_size = lax.axis_size("tp")
    reach = WINDOW // block
    hops = min(reach, ctx_size - 1)
    peers = max(tp_size - 1, 1)
    slice_width, width = window_of(model, tp_size)
    piece_width = -(-(width + query_width) // (LANES * ctx_size)) * LANES

    def kernel(*refs):
        layer_kernel((ctx_size, tp_size, reach, hops), *refs)

    whole = pl.BlockSpec(memory_space=pltpu.VMEM)
    in_specs = [whole] * 18
    in_specs[3] = pl.BlockSpec(memory_space=pltpu.SMEM)
    layer_out, grad_in, down, query, key, value, out_down, out_up = pl.pallas_call(
        kernel,
        out_shape=(
            jax.ShapeDtypeStruct((rows, model), bf16),
            jax.ShapeDtypeStruct((rows, model), bf16),
            jax.ShapeDtypeStruct((3 * rank, slice_width), f32),
            jax.ShapeDtypeStruct((rank, query_width), f32),
            jax.ShapeDtypeStruct((rank, head), f32),
            jax.ShapeDtypeStruct((rank, head), f32),
            jax.ShapeDtypeStruct((rank, query_width), f32),
            jax.ShapeDtypeStruct((rank, slice_width), f32),
        ),
        in_specs=in_specs,
        out_specs=(whole,) * 8,
        scratch_shapes=[
            pltpu.VMEM((1, model), f32),
            pltpu.VMEM((1, model), f32),
            pltpu.VMEM((block, model), bf16),
            pltpu.VMEM((hops + 1, 8, block), jnp.int32),
            pltpu.VMEM((hops + 1, block, 2 * head), bf16),
            pltpu.VMEM((hops + 1, block, query_width // head * block), bf16),
            pltpu.VMEM((block, query_width), bf16),
            pltpu.VMEM((peers, rows, model), bf16),
            pltpu.VMEM((peers, rows, model), bf16),
            pltpu.VMEM((peers, rows, LANES), bf16),
            pltpu.VMEM((peers, rows, LANES), bf16),
            pltpu.VMEM((rows, model), f32),
            pltpu.VMEM((block, model), bf16),
            pltpu.VMEM((block, 2 * LANES), bf16),
            pltpu.VMEM((hops, block, 2 * head), bf16),
            pltpu.VMEM((hops, block, 2 * head), bf16),
            pltpu.VMEM((block, query_width), f32),
            pltpu.VMEM((block, head), f32),
            pltpu.VMEM((block, query_width + 2 * head), bf16),
            pltpu.VMEM((block, LANES), f32),
            pltpu.VMEM((block, LANES), bf16),
            pltpu.VMEM((peers, block, LANES), bf16),
            pltpu.VMEM((peers, rows, model), bf16),
            pltpu.VMEM((peers, rows, model), bf16),
            pltpu.VMEM((rows, model), f32),
            pltpu.VMEM((ctx_size, 4 * rank, piece_width), bf16),
            pltpu.VMEM((ctx_size - 1, 4 * rank, piece_width), bf16),
            pltpu.VMEM((ctx_size, 4 * rank, piece_width), bf16),
            pltpu.SemaphoreType.DMA((2, peers)),
            pltpu.SemaphoreType.DMA((2, hops)),
            pltpu.SemaphoreType.DMA((2, hops)),
            pltpu.SemaphoreType.DMA((2, peers)),
            pltpu.SemaphoreType.DMA((2, peers)),
            pltpu.SemaphoreType.DMA((2, peers)),
            pltpu.SemaphoreType.DMA((2, peers)),
            pltpu.SemaphoreType.DMA((2, hops)),
            pltpu.SemaphoreType.DMA((2, peers)),
            pltpu.SemaphoreType.DMA((2, peers)),
            pltpu.SemaphoreType.DMA((2, ctx_size - 1)),
            pltpu.SemaphoreType.DMA((2, ctx_size - 1)),
        ],
        compiler_params=pltpu.CompilerParams(
            collective_id=0, has_side_effects=True, vmem_limit_bytes=56 * 1024 * 1024
        ),
    )(
        tokens,
        output_gradient,
        document_index.reshape(1, block),
        real_token_count,
        input_norm_gain,
        query_norm_gain.reshape(1, head),
        key_norm_gain.reshape(1, head),
        output_norm_gain,
        query_projection,
        key_projection,
        value_projection,
        output_projection,
        adapter_down_maps.T,
        adapter_query_up,
        adapter_key_up,
        adapter_value_up,
        adapter_output_down.T,
        adapter_output_up,
    )
    return layer_out, grad_in, down.T, query, key, value, out_down.T, out_up


def solution(mesh):
    in_specs = (
        P(("groups", "ctx", "tp"), None),
        P(("groups", "ctx", "tp"), None),
        P(("groups", "ctx")),
        P(("groups", "ctx")),
        P(),
        P(),
        P(),
        P(),
        P(None, "tp"),
        P(None, "tp"),
        P(None, "tp"),
        P("tp", None),
        P(),
        P(None, "tp"),
        P(None, "tp"),
        P(None, "tp"),
        P("tp", None),
        P(),
    )
    out_specs = (
        P(("groups", "ctx", "tp"), None),
        P(("groups", "ctx", "tp"), None),
        P(("groups", "tp"), None),
        P("groups", "tp"),
        P("groups", "tp"),
        P("groups", "tp"),
        P(("groups", "tp"), None),
        P("groups", "tp"),
    )
    return jax.shard_map(
        on_device, mesh=mesh, in_specs=in_specs, out_specs=out_specs, check_vma=False
    )
```

```python
import jax
import jax.numpy as jnp
from jax import lax
from jax.experimental import pallas as pl
from jax.experimental.pallas import tpu as pltpu
from jax.sharding import PartitionSpec as P

WINDOW = 1024
LANES = 128
NORM_ROWS = 32

epsilon = 1e-06
adapter_scale = 2.0
score_scale = 168.0 ** (-0.5)

bf16 = jnp.bfloat16
f32 = jnp.float32


def norm_rows(source, gain_vec):
    inverse = lax.rsqrt(jnp.mean(source * source, axis=-1, keepdims=True) + epsilon)
    return source * inverse * gain_vec


def norm_back(source, gain_vec, incoming):
    inverse = lax.rsqrt(jnp.mean(source * source, axis=-1, keepdims=True) + epsilon)
    scaled = source * inverse
    upward = incoming * gain_vec
    return inverse * (upward - scaled * jnp.mean(upward * scaled, axis=-1, keepdims=True))


def matrix_product(first_op, second_op):
    return jnp.dot(first_op, second_op, preferred_element_type=f32)


def multiply_by_transpose(first_op, second_op):
    return lax.dot_general(
        first_op, second_op, (((1,), (1,)), ((), ())), preferred_element_type=f32
    )


def window_of(model_width, tp_size):
    slice_width = model_width // tp_size
    if slice_width % LANES == 0:
        return slice_width, slice_width
    width = min(-(-(slice_width + LANES - 1) // LANES) * LANES, model_width)
    if tp_size == 2:
        width = -(-slice_width // LANES) * LANES
    return slice_width, width


def window_start(tp_index, slice_width, width, model_width):
    return jnp.minimum(tp_index * slice_width // LANES * LANES, model_width - width)


def layer_kernel(
    shapes,
    staged,
    tokens,
    output_gradient,
    documents,
    token_count,
    input_gain_vec,
    query_gain,
    key_gain,
    output_gain_vec,
    query_w,
    key_w,
    value_w,
    output_w,
    down_w,
    query_up,
    key_up,
    value_up,
    out_down,
    out_up,
    layer_out,
    grad_in,
    down_out_rows,
    query_up_out,
    key_up_out,
    value_up_out,
    out_down_out,
    out_up_out,
    input_gain,
    output_gain,
    normed,
    codes,
    pairs,
    weights,
    attended,
    out_send,
    out_recv,
    mid_send,
    mid_recv,
    pre_norm,
    grad_full,
    small_full,
    pair_grads,
    pair_recv,
    query_pre,
    key_pre,
    pre_grads,
    mid_pad,
    mid_grads,
    mid_grads_recv,
    normed_send,
    normed_recv,
    grad_normed,
    sums_send,
    sums_recv,
    sums_all,
    gather_sems,
    code_sems,
    pair_sems,
    out_sems,
    mid_sems,
    grad_sems,
    small_sems,
    back_sems,
    mid_grad_sems,
    normed_sems,
    sum_sems,
    total_sems,
):
    ctx_size, tp_size, reach, hops = shapes
    rows, model = tokens.shape
    chunk = min(NORM_ROWS, rows)
    block = documents.shape[1]
    head = key_w.shape[1]
    heads = query_w.shape[1] // head
    rank = key_up.shape[0]
    ctx = lax.axis_index("ctx")
    tp = lax.axis_index("tp")

    def tp_at(step):
        return lax.rem(tp + step, tp_size)

    def ctx_at(step):
        return lax.rem(ctx + step, ctx_size)

    def remote(source, target, sems, slot, where):
        return pltpu.make_async_remote_copy(
            src_ref=source,
            dst_ref=target,
            send_sem=sems.at[0, slot],
            recv_sem=sems.at[1, slot],
            device_id=where,
            device_id_type=pl.DeviceIdType.MESH,
        )

    def rows_of(index):
        return pl.ds(pl.multiple_of(index * rows, rows), rows)

    mine = rows_of(tp)

    barrier = pltpu.get_barrier_semaphore()
    for step in range(1, tp_size):
        pl.semaphore_signal(
            barrier, inc=1, device_id={"tp": tp_at(step)}, device_id_type=pl.DeviceIdType.MESH
        )
    for step in range(1, ctx_size):
        pl.semaphore_signal(
            barrier, inc=1, device_id={"ctx": ctx_at(step)}, device_id_type=pl.DeviceIdType.MESH
        )

    input_gain[...] = input_gain_vec[...].reshape(1, model)
    output_gain[...] = output_gain_vec[...].reshape(1, model)

    def norm_chunk(index, carry):
        at = pl.ds(pl.multiple_of(index * chunk, chunk), chunk)
        to = pl.ds(pl.multiple_of(tp * rows + index * chunk, chunk), chunk)
        normed[to, :] = norm_rows(tokens[at, :].astype(f32), input_gain[...]).astype(bf16)
        return carry

    staged[0].wait()
    lax.fori_loop(0, rows // chunk, norm_chunk, 0)

    lane_pos = lax.broadcasted_iota(jnp.int32, (1, block), 1)
    valid_lane = (lane_pos < token_count[0]).astype(f32)
    valid_sub = (
        lax.broadcasted_iota(jnp.int32, (block, 1), 0) < token_count[0]
    ).astype(f32)
    own_codes = jnp.where(lane_pos < token_count[0], documents[...] + 1, 0)
    codes[0] = jnp.broadcast_to(own_codes, codes.shape[1:])
    for hop in range(1, hops + 1):

        @pl.when(ctx < hop)
        def _(hop=hop):
            codes[hop] = jnp.zeros(codes.shape[1:], codes.dtype)
            pairs[hop] = jnp.zeros(pairs.shape[1:], pairs.dtype)

    odd = lax.rem(ctx, 2) == 1
    even = jnp.logical_not(odd)
    has_up = ctx + 2 < ctx_size
    partner = {"ctx": ctx + 1 - 2 * lax.rem(ctx, 2)}
    above = {"ctx": ctx_at(2)}
    below = {"ctx": ctx_at(ctx_size - 2)}
    arrives = (
        (even & (ctx >= 2)) | (odd & (ctx >= 5)),
        has_up & (ctx >= 2),
        even | (ctx >= 3),
        has_up,
    )
    sends = (
        (even & (ctx >= 4)) | (odd & (ctx >= 3)),
        ctx >= 4,
        odd | (ctx >= 2),
        ctx >= 2,
    )
    for place in range(4):

        @pl.when(jnp.logical_not(arrives[place]))
        def _(place=place):
            pair_recv[place] = jnp.zeros(pair_recv.shape[1:], pair_recv.dtype)

    pl.semaphore_wait(barrier, tp_size - 1 + ctx_size - 1)

    gathers = []
    for step in range(1, tp_size):
        copy = remote(
            normed.at[mine], normed.at[mine], gather_sems, step - 1, {"tp": tp_at(step)}
        )
        copy.start()
        gathers.append(copy)

    def code_copy(hop):
        return remote(codes.at[0], codes.at[hop], code_sems, hop - 1, {"ctx": ctx_at(hop)})

    def pair_copy(source, target, where):
        return remote(pairs.at[source], pairs.at[target], pair_sems, target - 1, where)

    def back_copy(hop, place, where):
        return remote(pair_grads.at[hop - 1], pair_recv.at[place], back_sems, place, where)

    pair_arrives = {1: odd | (ctx >= 2), 2: ctx >= 2, 3: ctx >= 3, 4: ctx >= 4}
    pair_arrives[3] = (odd & (ctx >= 3)) | (even & (ctx >= 4))

    for hop in range(1, hops + 1):

        @pl.when(ctx + hop < ctx_size)
        def _(hop=hop):
            code_copy(hop).start()

    for copy in gathers:
        copy.wait()

    for place in (9, 10, 8, 12):
        staged[place].wait()
    inputs = normed[...]
    middles = multiply_by_transpose(inputs, down_w[...]).astype(bf16)
    mid_pad[...] = jnp.zeros(mid_pad.shape, f32)
    mid_pad[:, : 3 * rank] = middles.astype(f32)

    def projected(weight, up, place):
        return matrix_product(inputs, weight[...]) + adapter_scale * matrix_product(
            middles[:, place * rank : (place + 1) * rank], up[...]
        )

    key_pre[...] = projected(key_w, key_up, 1)
    pairs[0, :, :head] = norm_rows(key_pre[...], key_gain[...]).astype(bf16)
    pairs[0, :, head:] = projected(value_w, value_up, 2).astype(bf16)

    @pl.when(has_up)
    def _():
        pair_copy(0, 2, above).start()

    @pl.when(even)
    def _():
        pair_copy(0, 1, partner).start()

    query_pre[...] = projected(query_w, query_up, 0)
    query_list = [
        norm_rows(query_pre[:, h * head : (h + 1) * head], query_gain[...]) for h in range(heads)
    ]
    query_rows = jnp.concatenate(query_list, axis=0).astype(bf16)
    query_cols = jnp.concatenate([q.T for q in query_list], axis=1).astype(bf16)

    sub = lax.broadcasted_iota(jnp.int32, (block, block), 0)
    lane = lax.broadcasted_iota(jnp.int32, (block, block), 1)
    wanted = (documents[...] + 1).astype(f32)
    totals = jnp.zeros((1, heads * block), f32)
    outputs = jnp.zeros((head, heads * block), f32)
    for hop in range(1, hops + 1):

        @pl.when(ctx >= hop)
        def _(hop=hop):
            code_copy(hop).wait_recv()

    def receive_pair(hop):
        @pl.when(pair_arrives[hop])
        def _():
            pair_copy(0, hop, partner).wait_recv()

    receive_pair(2)

    @pl.when(has_up & (ctx >= 2))
    def _():
        pair_copy(2, 4, above).start()

    @pl.when(even & (ctx >= 2))
    def _():
        pair_copy(2, 3, partner).start()

    @pl.when(odd & (ctx >= 2))
    def _():
        pair_copy(2, 1, partner).start()

    for hop in (0, 2, 1, 4, 3):
        if hop == 1:
            receive_pair(1)
            receive_pair(4)

            @pl.when(odd & (ctx >= 4))
            def _():
                pair_copy(4, 3, partner).start()

        if hop == 3:
            receive_pair(3)
        code_row = codes[hop][0:1, :].astype(f32)
        code_col = jnp.sum(jnp.where(sub == lane, code_row, 0.0), axis=1, keepdims=True)
        allowed = code_col == wanted
        if hop == 0:
            allowed = (sub == lane) | ((sub < lane) & allowed)
        if hop == reach:
            allowed = (sub > lane) & allowed
        allowed = allowed.astype(f32)
        allowed = jnp.concatenate([allowed] * heads, axis=1)
        scores = matrix_product(pairs[hop, :, :head], query_cols) * score_scale
        exps = jnp.where(allowed > 0.0, jnp.exp(scores), 0.0)
        totals = totals + jnp.sum(exps, axis=0, keepdims=True)
        exps = exps.astype(bf16)
        weights[hop] = exps
        values_cols = pairs[hop, :, head:].astype(f32).T.astype(bf16)
        outputs = outputs + matrix_product(values_cols, exps)
    inverse_totals = 1.0 / totals
    outputs = outputs * inverse_totals
    for h in range(heads):
        piece = outputs[:, h * block : (h + 1) * block] * valid_lane
        attended[:, h * head : (h + 1) * head] = piece.T.astype(bf16)

    staged[11].wait()
    mid_send[...] = jnp.zeros(mid_send.shape, bf16)
    out_copies = []
    for step in range(1, tp_size):
        theirs = attended[rows_of(tp_at(step)), :]
        mid_send[step - 1, :, :rank] = multiply_by_transpose(theirs, out_down[...]).astype(bf16)
        out_send[step - 1] = matrix_product(theirs, output_w[...]).astype(bf16)
        for source, target, sems in (
            (mid_send, mid_recv, mid_sems),
            (out_send, out_recv, out_sems),
        ):
            copy = remote(
                source.at[step - 1], target.at[step - 1], sems, step - 1, {"tp": tp_at(step)}
            )
            copy.start()
            out_copies.append(copy)
    own_rows = attended[mine, :]
    mid_sum = multiply_by_transpose(own_rows, out_down[...]).astype(bf16).astype(f32)
    pre_norm[...] = matrix_product(own_rows, output_w[...])
    for copy in out_copies:
        copy.wait()
    for step in range(1, tp_size):
        mid_sum = mid_sum + mid_recv[step - 1, :, :rank].astype(f32)
    mid_out = mid_sum.astype(bf16)
    pre_norm[...] += adapter_scale * matrix_product(mid_out, out_up[...])

    def out_chunk(index, carry):
        at = pl.ds(pl.multiple_of(index * chunk, chunk), chunk)
        to = pl.ds(pl.multiple_of(tp * rows + index * chunk, chunk), chunk)
        held = pre_norm[at, :]
        for step in range(1, tp_size):
            held = held + out_recv[step - 1, at, :].astype(f32)
        layer_out[at, :] = norm_rows(held, output_gain[...]).astype(bf16)
        grad_full[to, :] = norm_back(
            held, output_gain[...], output_gradient[at, :].astype(f32)
        ).astype(bf16)
        return carry

    staged[1].wait()
    lax.fori_loop(0, rows // chunk, out_chunk, 0)

    grad_copies = []
    for step in range(1, tp_size):
        copy = remote(
            grad_full.at[mine], grad_full.at[mine], grad_sems, step - 1, {"tp": tp_at(step)}
        )
        copy.start()
        grad_copies.append(copy)
    grad_mid_out = adapter_scale * multiply_by_transpose(grad_full[mine, :], out_up[...])
    small_full[mine, :] = jnp.zeros((rows, 2 * LANES), bf16)
    small_full[mine, :rank] = grad_mid_out.astype(bf16)
    small_full[mine, LANES : LANES + rank] = mid_out
    for step in range(1, tp_size):
        copy = remote(
            small_full.at[mine], small_full.at[mine], small_sems, step - 1, {"tp": tp_at(step)}
        )
        copy.start()
        grad_copies.append(copy)
    for copy in grad_copies:
        copy.wait()

    grad_att = (
        multiply_by_transpose(grad_full[...], output_w[...])
        + matrix_product(small_full[:, :rank], out_down[...])
    ) * valid_sub
    grad_cols = jnp.concatenate(
        [grad_att[:, h * head : (h + 1) * head].T for h in range(heads)], axis=1
    ).astype(bf16)
    grad_float = grad_cols.astype(f32)
    inner = jnp.sum(grad_float * outputs, axis=0, keepdims=True)
    grad_rows = (grad_float * inverse_totals).T.astype(bf16)
    row_scale = inverse_totals * score_scale

    query_back = jnp.zeros((head, heads * block), f32)
    odd_share = odd.astype(f32)
    even_share = 1.0 - odd_share

    def receive_back(place):
        @pl.when(arrives[place])
        def _():
            back_copy(1, place, partner).wait_recv()

    def send_back(hop, place, where, sends):
        @pl.when(sends)
        def _():
            back_copy(hop, place, where).start()

    for hop in (3, 4, 1, 2, 0):
        keys = pairs[hop, :, :head]
        exps = weights[hop]
        probs_back = matrix_product(pairs[hop, :, head:], grad_cols)
        scores_back = (exps.astype(f32) * ((probs_back - inner) * row_scale)).astype(bf16)
        keys_back = matrix_product(scores_back, query_rows)
        values_back = matrix_product(exps, grad_rows)
        query_back = query_back + matrix_product(keys.astype(f32).T.astype(bf16), scores_back)
        pair_back = jnp.concatenate([keys_back, values_back], axis=1)
        if hop == 3:
            pair_grads[2] = pair_back.astype(bf16)
            send_back(3, 0, partner, sends[0])
        if hop == 4:
            receive_back(0)
            pair_back = pair_back + odd_share * pair_recv[0].astype(f32)
            pair_grads[3] = pair_back.astype(bf16)
            send_back(4, 1, below, sends[1])
        if hop == 1:
            pair_grads[0] = pair_back.astype(bf16)
            send_back(1, 2, partner, sends[2])
        if hop == 2:
            receive_back(2)
            receive_back(1)
            pair_back = pair_back + even_share * pair_recv[0].astype(f32)
            pair_back = pair_back + odd_share * pair_recv[2].astype(f32)
            pair_back = pair_back + pair_recv[1].astype(f32)
            pair_grads[1] = pair_back.astype(bf16)
            send_back(2, 3, below, sends[3])
        if hop == 0:
            own_pair = pair_back + even_share * pair_recv[2].astype(f32)
    query_width = heads * head
    for h in range(heads):
        at = slice(h * head, (h + 1) * head)
        pre_grads[:, at] = norm_back(
            query_pre[:, at], query_gain[...], query_back[:, h * block : (h + 1) * block].T
        ).astype(bf16)
    receive_back(3)
    own_pair = own_pair + pair_recv[3].astype(f32)
    own_keys, own_values = own_pair[:, :head], own_pair[:, head:]
    key_at = slice(query_width, query_width + head)
    value_at = slice(query_width + head, query_width + 2 * head)
    pre_grads[:, key_at] = norm_back(key_pre[...], key_gain[...], own_keys).astype(bf16)
    pre_grads[:, value_at] = own_values.astype(bf16)

    mid_grads[...] = jnp.zeros(mid_grads.shape, bf16)
    for place, (at, up) in enumerate(
        ((slice(0, query_width), query_up), (key_at, key_up), (value_at, value_up))
    ):
        mid_grads[:, place * rank : (place + 1) * rank] = (
            adapter_scale * multiply_by_transpose(pre_grads[:, at], up[...])
        ).astype(bf16)
    last_copies = []
    for step in range(1, tp_size):
        copy = remote(
            mid_grads, mid_grads_recv.at[step - 1], mid_grad_sems, step - 1, {"tp": tp_at(step)}
        )
        copy.start()
        last_copies.append(copy)

    def input_part(which):
        grads = pre_grads[which, :]
        return (
            multiply_by_transpose(grads[:, :query_width], query_w[...])
            + multiply_by_transpose(grads[:, key_at], key_w[...])
            + multiply_by_transpose(grads[:, value_at], value_w[...])
            + matrix_product(mid_grads[which, : 3 * rank], down_w[...])
        )

    slice_width, width = window_of(model, tp_size)
    start = window_start(tp, slice_width, width, model)
    window = pl.ds(pl.multiple_of(start, LANES), width)
    for copy in last_copies:
        copy.wait()
    mid_total = mid_grads[...].astype(f32)
    for step in range(1, tp_size):
        mid_total = mid_total + mid_grads_recv[step - 1].astype(f32)
    mid_total = mid_total.T[: 3 * rank].astype(bf16)
    middle_cols = mid_pad[...].T[: 3 * rank].astype(bf16)
    small_cols = small_full[...].astype(f32).T
    grad_mid_cols = small_cols[:rank].astype(bf16)
    mid_out_cols = small_cols[LANES : LANES + rank].astype(bf16)
    main_terms = jnp.concatenate(
        [
            matrix_product(mid_total, normed[:, window]),
            adapter_scale * matrix_product(mid_out_cols, grad_full[:, window]),
        ],
        axis=0,
    ).astype(bf16)
    up_terms = [
        adapter_scale * matrix_product(middle_cols[:rank], pre_grads[:, :query_width]),
        adapter_scale
        * jnp.concatenate(
            [
                matrix_product(middle_cols[rank : 2 * rank], pre_grads[:, key_at]),
                matrix_product(middle_cols[2 * rank :], pre_grads[:, value_at]),
            ],
            axis=1,
        ),
        matrix_product(grad_mid_cols, attended[...]),
        jnp.zeros((rank, query_width), f32),
    ]
    piece_width = sums_send.shape[2]
    padding = piece_width * ctx_size - width - query_width
    pieces = [main_terms, jnp.concatenate(up_terms, axis=0).astype(bf16)]
    if padding > 0:
        pieces.append(jnp.zeros((4 * rank, padding), bf16))
    every_term = jnp.concatenate(pieces, axis=1)
    for index in range(ctx_size):
        sums_send[index] = every_term[:, index * piece_width : (index + 1) * piece_width]
    sum_copies = []
    for step in range(1, ctx_size):
        copy = remote(
            sums_send.at[ctx_at(step)],
            sums_recv.at[step - 1],
            sum_sems,
            step - 1,
            {"ctx": ctx_at(step)},
        )
        copy.start()
        sum_copies.append(copy)

    normed_copies = []
    for step in range(1, tp_size):
        normed_send[step - 1] = input_part(rows_of(tp_at(step))).astype(bf16)
        copy = remote(
            normed_send.at[step - 1],
            normed_recv.at[step - 1],
            normed_sems,
            step - 1,
            {"tp": tp_at(step)},
        )
        copy.start()
        normed_copies.append(copy)

    grad_normed[...] = input_part(mine)
    for copy in sum_copies:
        copy.wait()
    total = sums_send[ctx].astype(f32)
    for step in range(1, ctx_size):
        total = total + sums_recv[step - 1].astype(f32)
    sums_all[ctx] = total.astype(bf16)
    total_copies = []
    for step in range(1, ctx_size):
        copy = remote(
            sums_all.at[ctx], sums_all.at[ctx], total_sems, step - 1, {"ctx": ctx_at(step)}
        )
        copy.start()
        total_copies.append(copy)

    for copy in normed_copies:
        copy.wait()

    def in_chunk(index, carry):
        at = pl.ds(pl.multiple_of(index * chunk, chunk), chunk)
        incoming = grad_normed[at, :]
        for step in range(1, tp_size):
            incoming = incoming + normed_recv[step - 1, at, :].astype(f32)
        grad_in[at, :] = norm_back(
            tokens[at, :].astype(f32), input_gain[...], incoming
        ).astype(bf16)
        return carry

    lax.fori_loop(0, rows // chunk, in_chunk, 0)

    for copy in total_copies:
        copy.wait()
    sums = jnp.concatenate([sums_all[index].astype(f32) for index in range(ctx_size)], axis=1)
    offset = tp * slice_width - start
    share = pltpu.roll(sums[:, :width], lax.rem(width - offset, width), 1)[:, :slice_width]
    ups = sums[:, width : width + query_width]
    down_out_rows[...] = share[: 3 * rank]
    out_up_out[...] = share[3 * rank :]
    query_up_out[...] = ups[:rank]
    key_up_out[...] = ups[rank : 2 * rank, :head]
    value_up_out[...] = ups[rank : 2 * rank, head : 2 * head]
    out_down_out[...] = ups[2 * rank : 3 * rank]

    for hop in range(1, hops + 1):

        @pl.when(ctx + hop < ctx_size)
        def _(hop=hop):
            code_copy(hop).wait_send()

    for target, sent in (
        (1, even | (ctx >= 2)),
        (2, has_up),
        (3, (even & (ctx >= 2)) | (odd & (ctx >= 4))),
        (4, has_up & (ctx >= 2)),
    ):

        @pl.when(sent)
        def _(target=target):
            pair_copy(0, target, partner).wait_send()

    for place in range(4):

        @pl.when(sends[place])
        def _(place=place):
            back_copy(1, place, partner).wait_send()


def on_device(
    tokens,
    output_gradient,
    document_index,
    real_token_count,
    input_norm_gain,
    query_norm_gain,
    key_norm_gain,
    output_norm_gain,
    query_projection,
    key_projection,
    value_projection,
    output_projection,
    adapter_down_maps,
    adapter_query_up,
    adapter_key_up,
    adapter_value_up,
    adapter_output_down,
    adapter_output_up,
):
    rows, model = tokens.shape
    block = document_index.shape[0]
    head = key_projection.shape[1]
    query_width = query_projection.shape[1]
    rank = adapter_key_up.shape[0]
    ctx_size = lax.axis_size("ctx")
    tp_size = lax.axis_size("tp")
    reach = WINDOW // block
    hops = min(reach, ctx_size - 1)
    peers = max(tp_size - 1, 1)
    slice_width, width = window_of(model, tp_size)
    piece_width = -(-(width + query_width) // (LANES * ctx_size)) * LANES

    order = (0, 9, 10, 8, 12, 11, 1)
    arguments = (
        tokens,
        output_gradient,
        document_index.reshape(1, block),
        real_token_count,
        input_norm_gain,
        query_norm_gain.reshape(1, head),
        key_norm_gain.reshape(1, head),
        output_norm_gain,
        query_projection,
        key_projection,
        value_projection,
        output_projection,
        adapter_down_maps.T,
        adapter_query_up,
        adapter_key_up,
        adapter_value_up,
        adapter_output_down.T,
        adapter_output_up,
    )

    def kernel(*refs):
        inputs, results = list(refs[:18]), refs[18:26]
        buffers, sems, scratch = refs[26 : 26 + len(order)], refs[26 + len(order)], refs[27 + len(order) :]
        staged = {}
        for slot, place in enumerate(order):
            staged[place] = pltpu.make_async_copy(inputs[place], buffers[slot], sems.at[slot])
            staged[place].start()
            inputs[place] = buffers[slot]
        layer_kernel((ctx_size, tp_size, reach, hops), staged, *inputs, *results, *scratch)

    def copy_results(*refs):
        copies = [
            pltpu.make_async_copy(refs[place], refs[8 + place], refs[16].at[place])
            for place in range(8)
        ]
        for copy in copies:
            copy.start()
        for copy in copies:
            copy.wait()

    whole = pl.BlockSpec(memory_space=pltpu.VMEM)
    in_specs = [whole] * 18
    in_specs[3] = pl.BlockSpec(memory_space=pltpu.SMEM)
    for place in order:
        in_specs[place] = pl.BlockSpec(memory_space=pl.ANY)
    out_shape = (
        jax.ShapeDtypeStruct((rows, model), bf16),
        jax.ShapeDtypeStruct((rows, model), bf16),
        jax.ShapeDtypeStruct((3 * rank, slice_width), f32),
        jax.ShapeDtypeStruct((rank, query_width), f32),
        jax.ShapeDtypeStruct((rank, head), f32),
        jax.ShapeDtypeStruct((rank, head), f32),
        jax.ShapeDtypeStruct((rank, query_width), f32),
        jax.ShapeDtypeStruct((rank, slice_width), f32),
    )
    results = pl.pallas_call(
        kernel,
        out_shape=out_shape,
        in_specs=in_specs,
        out_specs=(whole,) * 8,
        scratch_shapes=[
            *[pltpu.VMEM(arguments[place].shape, arguments[place].dtype) for place in order],
            pltpu.SemaphoreType.DMA((len(order),)),
            pltpu.VMEM((1, model), f32),
            pltpu.VMEM((1, model), f32),
            pltpu.VMEM((block, model), bf16),
            pltpu.VMEM((hops + 1, 8, block), jnp.int32),
            pltpu.VMEM((hops + 1, block, 2 * head), bf16),
            pltpu.VMEM((hops + 1, block, query_width // head * block), bf16),
            pltpu.VMEM((block, query_width), bf16),
            pltpu.VMEM((peers, rows, model), bf16),
            pltpu.VMEM((peers, rows, model), bf16),
            pltpu.VMEM((peers, rows, LANES), bf16),
            pltpu.VMEM((peers, rows, LANES), bf16),
            pltpu.VMEM((rows, model), f32),
            pltpu.VMEM((block, model), bf16),
            pltpu.VMEM((block, 2 * LANES), bf16),
            pltpu.VMEM((hops, block, 2 * head), bf16),
            pltpu.VMEM((hops, block, 2 * head), bf16),
            pltpu.VMEM((block, query_width), f32),
            pltpu.VMEM((block, head), f32),
            pltpu.VMEM((block, query_width + 2 * head), bf16),
            pltpu.VMEM((block, LANES), f32),
            pltpu.VMEM((block, LANES), bf16),
            pltpu.VMEM((peers, block, LANES), bf16),
            pltpu.VMEM((peers, rows, model), bf16),
            pltpu.VMEM((peers, rows, model), bf16),
            pltpu.VMEM((rows, model), f32),
            pltpu.VMEM((ctx_size, 4 * rank, piece_width), bf16),
            pltpu.VMEM((ctx_size - 1, 4 * rank, piece_width), bf16),
            pltpu.VMEM((ctx_size, 4 * rank, piece_width), bf16),
            pltpu.SemaphoreType.DMA((2, peers)),
            pltpu.SemaphoreType.DMA((2, hops)),
            pltpu.SemaphoreType.DMA((2, hops)),
            pltpu.SemaphoreType.DMA((2, peers)),
            pltpu.SemaphoreType.DMA((2, peers)),
            pltpu.SemaphoreType.DMA((2, peers)),
            pltpu.SemaphoreType.DMA((2, peers)),
            pltpu.SemaphoreType.DMA((2, hops)),
            pltpu.SemaphoreType.DMA((2, peers)),
            pltpu.SemaphoreType.DMA((2, peers)),
            pltpu.SemaphoreType.DMA((2, ctx_size - 1)),
            pltpu.SemaphoreType.DMA((2, ctx_size - 1)),
        ],
        compiler_params=pltpu.CompilerParams(
            collective_id=0, has_side_effects=True, vmem_limit_bytes=56 * 1024 * 1024
        ),
    )(*arguments)
    anywhere = pl.BlockSpec(memory_space=pl.ANY)
    layer_out, grad_in, down, query, key, value, out_down, out_up = pl.pallas_call(
        copy_results,
        out_shape=out_shape,
        in_specs=[anywhere] * 8,
        out_specs=(anywhere,) * 8,
        scratch_shapes=[pltpu.SemaphoreType.DMA((8,))],
        compiler_params=pltpu.CompilerParams(vmem_limit_bytes=60 * 1024 * 1024),
    )(*results)
    return layer_out, grad_in, down.T, query, key, value, out_down.T, out_up


def solution(mesh):
    in_specs = (
        P(("groups", "ctx", "tp"), None),
        P(("groups", "ctx", "tp"), None),
        P(("groups", "ctx")),
        P(("groups", "ctx")),
        P(),
        P(),
        P(),
        P(),
        P(None, "tp"),
        P(None, "tp"),
        P(None, "tp"),
        P("tp", None),
        P(),
        P(None, "tp"),
        P(None, "tp"),
        P(None, "tp"),
        P("tp", None),
        P(),
    )
    out_specs = (
        P(("groups", "ctx", "tp"), None),
        P(("groups", "ctx", "tp"), None),
        P(("groups", "tp"), None),
        P("groups", "tp"),
        P("groups", "tp"),
        P("groups", "tp"),
        P(("groups", "tp"), None),
        P("groups", "tp"),
    )
    return jax.shard_map(
        on_device, mesh=mesh, in_specs=in_specs, out_specs=out_specs, check_vma=False
    )
```

```python
import jax
import jax.numpy as jnp
from jax import lax
from jax.experimental import pallas as pl
from jax.experimental.pallas import tpu as pltpu
from jax.sharding import PartitionSpec as P

WINDOW = 1024
LANES = 128
NORM_ROWS = 32

epsilon = 1e-06
adapter_scale = 2.0
score_scale = 168.0 ** (-0.5)

bf16 = jnp.bfloat16
f32 = jnp.float32


def norm_rows(source, gain_vec):
    inverse = lax.rsqrt(jnp.mean(source * source, axis=-1, keepdims=True) + epsilon)
    return source * inverse * gain_vec


def norm_back(source, gain_vec, incoming):
    inverse = lax.rsqrt(jnp.mean(source * source, axis=-1, keepdims=True) + epsilon)
    scaled = source * inverse
    upward = incoming * gain_vec
    return inverse * (upward - scaled * jnp.mean(upward * scaled, axis=-1, keepdims=True))


def matrix_product(first_op, second_op):
    return jnp.dot(first_op, second_op, preferred_element_type=f32)


def multiply_by_transpose(first_op, second_op):
    return lax.dot_general(
        first_op, second_op, (((1,), (1,)), ((), ())), preferred_element_type=f32
    )


def window_of(model_width, tp_size):
    slice_width = model_width // tp_size
    if slice_width % LANES == 0:
        return slice_width, slice_width
    width = min(-(-(slice_width + LANES - 1) // LANES) * LANES, model_width)
    if tp_size == 2:
        width = -(-slice_width // LANES) * LANES
    return slice_width, width


def window_start(tp_index, slice_width, width, model_width):
    return jnp.minimum(tp_index * slice_width // LANES * LANES, model_width - width)


def layer_kernel(
    shapes,
    staged,
    tokens,
    output_gradient,
    documents,
    token_count,
    input_gain_vec,
    query_gain,
    key_gain,
    output_gain_vec,
    query_w,
    key_w,
    value_w,
    output_w,
    down_w,
    query_up,
    key_up,
    value_up,
    out_down,
    out_up,
    layer_out,
    grad_in,
    down_out_rows,
    query_up_out,
    key_up_out,
    value_up_out,
    out_down_out,
    out_up_out,
    input_gain,
    output_gain,
    normed,
    codes,
    pairs,
    weights,
    attended,
    out_send,
    out_recv,
    mid_send,
    mid_recv,
    pre_norm,
    grad_full,
    small_full,
    pair_grads,
    pair_recv,
    query_pre,
    key_pre,
    pre_grads,
    mid_pad,
    mid_grads,
    mid_grads_recv,
    normed_send,
    normed_recv,
    grad_normed,
    sums_send,
    sums_recv,
    sums_all,
    gather_sems,
    code_sems,
    pair_sems,
    out_sems,
    mid_sems,
    grad_sems,
    small_sems,
    back_sems,
    mid_grad_sems,
    normed_sems,
    sum_sems,
    total_sems,
):
    ctx_size, tp_size, reach, hops = shapes
    rows, model = tokens.shape
    chunk = min(NORM_ROWS, rows)
    block = documents.shape[1]
    head = key_w.shape[1]
    heads = query_w.shape[1] // head
    rank = key_up.shape[0]
    ctx = lax.axis_index("ctx")
    tp = lax.axis_index("tp")

    def tp_at(step):
        return lax.rem(tp + step, tp_size)

    def ctx_at(step):
        return lax.rem(ctx + step, ctx_size)

    def remote(source, target, sems, slot, where):
        return pltpu.make_async_remote_copy(
            src_ref=source,
            dst_ref=target,
            send_sem=sems.at[0, slot],
            recv_sem=sems.at[1, slot],
            device_id=where,
            device_id_type=pl.DeviceIdType.MESH,
        )

    def rows_of(index):
        return pl.ds(pl.multiple_of(index * rows, rows), rows)

    mine = rows_of(tp)

    barrier = pltpu.get_barrier_semaphore()
    for step in range(1, tp_size):
        pl.semaphore_signal(
            barrier, inc=1, device_id={"tp": tp_at(step)}, device_id_type=pl.DeviceIdType.MESH
        )
    for step in range(1, ctx_size):
        pl.semaphore_signal(
            barrier, inc=1, device_id={"ctx": ctx_at(step)}, device_id_type=pl.DeviceIdType.MESH
        )

    input_gain[...] = input_gain_vec[...].reshape(1, model)
    output_gain[...] = output_gain_vec[...].reshape(1, model)

    def norm_chunk(index, carry):
        at = pl.ds(pl.multiple_of(index * chunk, chunk), chunk)
        to = pl.ds(pl.multiple_of(tp * rows + index * chunk, chunk), chunk)
        normed[to, :] = norm_rows(tokens[at, :].astype(f32), input_gain[...]).astype(bf16)
        return carry

    staged[0].wait()
    lax.fori_loop(0, rows // chunk, norm_chunk, 0)

    lane_pos = lax.broadcasted_iota(jnp.int32, (1, block), 1)
    valid_lane = (lane_pos < token_count[0]).astype(f32)
    valid_sub = (
        lax.broadcasted_iota(jnp.int32, (block, 1), 0) < token_count[0]
    ).astype(f32)
    own_codes = jnp.where(lane_pos < token_count[0], documents[...] + 1, 0)
    codes[0] = jnp.broadcast_to(own_codes, codes.shape[1:])
    for hop in range(1, hops + 1):

        @pl.when(ctx < hop)
        def _(hop=hop):
            codes[hop] = jnp.zeros(codes.shape[1:], codes.dtype)
            pairs[hop] = jnp.zeros(pairs.shape[1:], pairs.dtype)

    odd = lax.rem(ctx, 2) == 1
    even = jnp.logical_not(odd)
    has_up = ctx + 2 < ctx_size
    partner = {"ctx": ctx + 1 - 2 * lax.rem(ctx, 2)}
    above = {"ctx": ctx_at(2)}
    below = {"ctx": ctx_at(ctx_size - 2)}
    arrives = (
        (even & (ctx >= 2)) | (odd & (ctx >= 5)),
        has_up & (ctx >= 2),
        even | (ctx >= 3),
        has_up,
    )
    sends = (
        (even & (ctx >= 4)) | (odd & (ctx >= 3)),
        ctx >= 4,
        odd | (ctx >= 2),
        ctx >= 2,
    )
    for place in range(4):

        @pl.when(jnp.logical_not(arrives[place]))
        def _(place=place):
            pair_recv[place] = jnp.zeros(pair_recv.shape[1:], pair_recv.dtype)

    pl.semaphore_wait(barrier, tp_size - 1 + ctx_size - 1)

    gathers = []
    for step in range(1, tp_size):
        copy = remote(
            normed.at[mine], normed.at[mine], gather_sems, step - 1, {"tp": tp_at(step)}
        )
        copy.start()
        gathers.append(copy)

    def code_copy(hop):
        return remote(codes.at[0], codes.at[hop], code_sems, hop - 1, {"ctx": ctx_at(hop)})

    def pair_copy(source, target, where):
        return remote(pairs.at[source], pairs.at[target], pair_sems, target - 1, where)

    def back_copy(hop, place, where):
        return remote(pair_grads.at[hop - 1], pair_recv.at[place], back_sems, place, where)

    pair_arrives = {1: odd | (ctx >= 2), 2: ctx >= 2, 3: ctx >= 3, 4: ctx >= 4}
    pair_arrives[3] = (odd & (ctx >= 3)) | (even & (ctx >= 4))

    for hop in range(1, hops + 1):

        @pl.when(ctx + hop < ctx_size)
        def _(hop=hop):
            code_copy(hop).start()

    for copy in gathers:
        copy.wait()

    for place in (9, 10, 8, 12):
        staged[place].wait()
    inputs = normed[...]
    middles = multiply_by_transpose(inputs, down_w[...]).astype(bf16)
    mid_pad[...] = jnp.zeros(mid_pad.shape, f32)
    mid_pad[:, : 3 * rank] = middles.astype(f32)

    def projected(weight, up, place):
        return matrix_product(inputs, weight[...]) + adapter_scale * matrix_product(
            middles[:, place * rank : (place + 1) * rank], up[...]
        )

    key_pre[...] = projected(key_w, key_up, 1)
    pairs[0, :, :head] = norm_rows(key_pre[...], key_gain[...]).astype(bf16)
    pairs[0, :, head:] = projected(value_w, value_up, 2).astype(bf16)

    @pl.when(has_up)
    def _():
        pair_copy(0, 2, above).start()

    @pl.when(even)
    def _():
        pair_copy(0, 1, partner).start()

    query_pre[...] = projected(query_w, query_up, 0)
    query_list = [
        norm_rows(query_pre[:, h * head : (h + 1) * head], query_gain[...]) for h in range(heads)
    ]
    query_rows = jnp.concatenate(query_list, axis=0).astype(bf16)
    query_cols = jnp.concatenate([q.T for q in query_list], axis=1).astype(bf16)

    sub = lax.broadcasted_iota(jnp.int32, (block, block), 0)
    lane = lax.broadcasted_iota(jnp.int32, (block, block), 1)
    wanted = (documents[...] + 1).astype(f32)
    totals = jnp.zeros((1, heads * block), f32)
    outputs = jnp.zeros((head, heads * block), f32)
    for hop in range(1, hops + 1):

        @pl.when(ctx >= hop)
        def _(hop=hop):
            code_copy(hop).wait_recv()

    def receive_pair(hop):
        @pl.when(pair_arrives[hop])
        def _():
            pair_copy(0, hop, partner).wait_recv()

    receive_pair(2)

    @pl.when(has_up & (ctx >= 2))
    def _():
        pair_copy(2, 4, above).start()

    @pl.when(even & (ctx >= 2))
    def _():
        pair_copy(2, 3, partner).start()

    @pl.when(odd & (ctx >= 2))
    def _():
        pair_copy(2, 1, partner).start()

    for hop in (0, 2, 1, 4, 3):
        if hop == 1:
            receive_pair(1)
            receive_pair(4)

            @pl.when(odd & (ctx >= 4))
            def _():
                pair_copy(4, 3, partner).start()

        if hop == 3:
            receive_pair(3)
        code_row = codes[hop][0:1, :].astype(f32)
        code_col = jnp.sum(jnp.where(sub == lane, code_row, 0.0), axis=1, keepdims=True)
        allowed = code_col == wanted
        if hop == 0:
            allowed = (sub == lane) | ((sub < lane) & allowed)
        if hop == reach:
            allowed = (sub > lane) & allowed
        allowed = allowed.astype(f32)
        allowed = jnp.concatenate([allowed] * heads, axis=1)
        scores = matrix_product(pairs[hop, :, :head], query_cols) * score_scale
        exps = jnp.where(allowed > 0.0, jnp.exp(scores), 0.0)
        totals = totals + jnp.sum(exps, axis=0, keepdims=True)
        exps = exps.astype(bf16)
        weights[hop] = exps
        values_cols = pairs[hop, :, head:].astype(f32).T.astype(bf16)
        outputs = outputs + matrix_product(values_cols, exps)
    inverse_totals = 1.0 / totals
    outputs = outputs * inverse_totals
    for h in range(heads):
        piece = outputs[:, h * block : (h + 1) * block] * valid_lane
        attended[:, h * head : (h + 1) * head] = piece.T.astype(bf16)

    staged[11].wait()
    mid_send[...] = jnp.zeros(mid_send.shape, bf16)
    out_copies = []
    for step in range(1, tp_size):
        theirs = attended[rows_of(tp_at(step)), :]
        mid_send[step - 1, :, :rank] = multiply_by_transpose(theirs, out_down[...]).astype(bf16)
        out_send[step - 1] = matrix_product(theirs, output_w[...]).astype(bf16)
        for source, target, sems in (
            (mid_send, mid_recv, mid_sems),
            (out_send, out_recv, out_sems),
        ):
            copy = remote(
                source.at[step - 1], target.at[step - 1], sems, step - 1, {"tp": tp_at(step)}
            )
            copy.start()
            out_copies.append(copy)
    own_rows = attended[mine, :]
    mid_sum = multiply_by_transpose(own_rows, out_down[...]).astype(bf16).astype(f32)
    pre_norm[...] = matrix_product(own_rows, output_w[...])
    for copy in out_copies:
        copy.wait()
    for step in range(1, tp_size):
        mid_sum = mid_sum + mid_recv[step - 1, :, :rank].astype(f32)
    mid_out = mid_sum.astype(bf16)
    pre_norm[...] += adapter_scale * matrix_product(mid_out, out_up[...])

    def out_chunk(index, carry):
        at = pl.ds(pl.multiple_of(index * chunk, chunk), chunk)
        to = pl.ds(pl.multiple_of(tp * rows + index * chunk, chunk), chunk)
        held = pre_norm[at, :]
        for step in range(1, tp_size):
            held = held + out_recv[step - 1, at, :].astype(f32)
        layer_out[at, :] = norm_rows(held, output_gain[...]).astype(bf16)
        grad_full[to, :] = norm_back(
            held, output_gain[...], output_gradient[at, :].astype(f32)
        ).astype(bf16)
        return carry

    staged[1].wait()
    lax.fori_loop(0, rows // chunk, out_chunk, 0)

    grad_copies = []
    for step in range(1, tp_size):
        copy = remote(
            grad_full.at[mine], grad_full.at[mine], grad_sems, step - 1, {"tp": tp_at(step)}
        )
        copy.start()
        grad_copies.append(copy)
    grad_mid_out = adapter_scale * multiply_by_transpose(grad_full[mine, :], out_up[...])
    small_full[mine, :] = jnp.zeros((rows, 2 * LANES), bf16)
    small_full[mine, :rank] = grad_mid_out.astype(bf16)
    small_full[mine, LANES : LANES + rank] = mid_out
    for step in range(1, tp_size):
        copy = remote(
            small_full.at[mine], small_full.at[mine], small_sems, step - 1, {"tp": tp_at(step)}
        )
        copy.start()
        grad_copies.append(copy)
    for copy in grad_copies:
        copy.wait()

    grad_att = (
        multiply_by_transpose(grad_full[...], output_w[...])
        + matrix_product(small_full[:, :rank], out_down[...])
    ) * valid_sub
    grad_cols = jnp.concatenate(
        [grad_att[:, h * head : (h + 1) * head].T for h in range(heads)], axis=1
    ).astype(bf16)
    grad_float = grad_cols.astype(f32)
    inner = jnp.sum(grad_float * outputs, axis=0, keepdims=True)
    grad_rows = (grad_float * inverse_totals).T.astype(bf16)
    row_scale = inverse_totals * score_scale

    query_back = jnp.zeros((head, heads * block), f32)
    odd_share = odd.astype(f32)
    even_share = 1.0 - odd_share

    def receive_back(place):
        @pl.when(arrives[place])
        def _():
            back_copy(1, place, partner).wait_recv()

    def send_back(hop, place, where, sends):
        @pl.when(sends)
        def _():
            back_copy(hop, place, where).start()

    for hop in (3, 4, 1, 2, 0):
        keys = pairs[hop, :, :head]
        exps = weights[hop]
        probs_back = matrix_product(pairs[hop, :, head:], grad_cols)
        scores_back = (exps.astype(f32) * ((probs_back - inner) * row_scale)).astype(bf16)
        keys_back = matrix_product(scores_back, query_rows)
        values_back = matrix_product(exps, grad_rows)
        query_back = query_back + matrix_product(keys.astype(f32).T.astype(bf16), scores_back)
        pair_back = jnp.concatenate([keys_back, values_back], axis=1)
        if hop == 3:
            pair_grads[2] = pair_back.astype(bf16)
            send_back(3, 0, partner, sends[0])
        if hop == 4:
            receive_back(0)
            pair_back = pair_back + odd_share * pair_recv[0].astype(f32)
            pair_grads[3] = pair_back.astype(bf16)
            send_back(4, 1, below, sends[1])
        if hop == 1:
            pair_grads[0] = pair_back.astype(bf16)
            send_back(1, 2, partner, sends[2])
        if hop == 2:
            receive_back(2)
            receive_back(1)
            pair_back = pair_back + even_share * pair_recv[0].astype(f32)
            pair_back = pair_back + odd_share * pair_recv[2].astype(f32)
            pair_back = pair_back + pair_recv[1].astype(f32)
            pair_grads[1] = pair_back.astype(bf16)
            send_back(2, 3, below, sends[3])
        if hop == 0:
            own_pair = pair_back + even_share * pair_recv[2].astype(f32)
    query_width = heads * head
    for h in range(heads):
        at = slice(h * head, (h + 1) * head)
        pre_grads[:, at] = norm_back(
            query_pre[:, at], query_gain[...], query_back[:, h * block : (h + 1) * block].T
        ).astype(bf16)
    receive_back(3)
    own_pair = own_pair + pair_recv[3].astype(f32)
    own_keys, own_values = own_pair[:, :head], own_pair[:, head:]
    key_at = slice(query_width, query_width + head)
    value_at = slice(query_width + head, query_width + 2 * head)
    pre_grads[:, key_at] = norm_back(key_pre[...], key_gain[...], own_keys).astype(bf16)
    pre_grads[:, value_at] = own_values.astype(bf16)

    mid_grads[...] = jnp.zeros(mid_grads.shape, bf16)
    for place, (at, up) in enumerate(
        ((slice(0, query_width), query_up), (key_at, key_up), (value_at, value_up))
    ):
        mid_grads[:, place * rank : (place + 1) * rank] = (
            adapter_scale * multiply_by_transpose(pre_grads[:, at], up[...])
        ).astype(bf16)
    last_copies = []
    for step in range(1, tp_size):
        copy = remote(
            mid_grads, mid_grads_recv.at[step - 1], mid_grad_sems, step - 1, {"tp": tp_at(step)}
        )
        copy.start()
        last_copies.append(copy)

    def input_part(which):
        grads = pre_grads[which, :]
        return (
            multiply_by_transpose(grads[:, :query_width], query_w[...])
            + multiply_by_transpose(grads[:, key_at], key_w[...])
            + multiply_by_transpose(grads[:, value_at], value_w[...])
            + matrix_product(mid_grads[which, : 3 * rank], down_w[...])
        )

    slice_width, width = window_of(model, tp_size)
    start = window_start(tp, slice_width, width, model)
    window = pl.ds(pl.multiple_of(start, LANES), width)
    for copy in last_copies:
        copy.wait()
    mid_total = mid_grads[...].astype(f32)
    for step in range(1, tp_size):
        mid_total = mid_total + mid_grads_recv[step - 1].astype(f32)
    mid_total = mid_total.T[: 3 * rank].astype(bf16)
    middle_cols = mid_pad[...].T[: 3 * rank].astype(bf16)
    small_cols = small_full[...].astype(f32).T
    grad_mid_cols = small_cols[:rank].astype(bf16)
    mid_out_cols = small_cols[LANES : LANES + rank].astype(bf16)
    main_terms = jnp.concatenate(
        [
            matrix_product(mid_total, normed[:, window]),
            adapter_scale * matrix_product(mid_out_cols, grad_full[:, window]),
        ],
        axis=0,
    ).astype(bf16)
    up_terms = [
        adapter_scale * matrix_product(middle_cols[:rank], pre_grads[:, :query_width]),
        adapter_scale
        * jnp.concatenate(
            [
                matrix_product(middle_cols[rank : 2 * rank], pre_grads[:, key_at]),
                matrix_product(middle_cols[2 * rank :], pre_grads[:, value_at]),
            ],
            axis=1,
        ),
        matrix_product(grad_mid_cols, attended[...]),
        jnp.zeros((rank, query_width), f32),
    ]
    piece_width = sums_send.shape[2]
    padding = piece_width * ctx_size - width - query_width
    pieces = [main_terms, jnp.concatenate(up_terms, axis=0).astype(bf16)]
    if padding > 0:
        pieces.append(jnp.zeros((4 * rank, padding), bf16))
    every_term = jnp.concatenate(pieces, axis=1)
    for index in range(ctx_size):
        sums_send[index] = every_term[:, index * piece_width : (index + 1) * piece_width]
    sum_copies = []
    for step in range(1, ctx_size):
        copy = remote(
            sums_send.at[ctx_at(step)],
            sums_recv.at[step - 1],
            sum_sems,
            step - 1,
            {"ctx": ctx_at(step)},
        )
        copy.start()
        sum_copies.append(copy)

    normed_copies = []
    for step in range(1, tp_size):
        normed_send[step - 1] = input_part(rows_of(tp_at(step))).astype(bf16)
        copy = remote(
            normed_send.at[step - 1],
            normed_recv.at[step - 1],
            normed_sems,
            step - 1,
            {"tp": tp_at(step)},
        )
        copy.start()
        normed_copies.append(copy)

    grad_normed[...] = input_part(mine)
    for copy in sum_copies:
        copy.wait()
    total = sums_send[ctx].astype(f32)
    for step in range(1, ctx_size):
        total = total + sums_recv[step - 1].astype(f32)
    sums_all[ctx] = total.astype(bf16)
    total_copies = []
    for step in range(1, ctx_size):
        copy = remote(
            sums_all.at[ctx], sums_all.at[ctx], total_sems, step - 1, {"ctx": ctx_at(step)}
        )
        copy.start()
        total_copies.append(copy)

    for copy in normed_copies:
        copy.wait()

    def in_chunk(index, carry):
        at = pl.ds(pl.multiple_of(index * chunk, chunk), chunk)
        incoming = grad_normed[at, :]
        for step in range(1, tp_size):
            incoming = incoming + normed_recv[step - 1, at, :].astype(f32)
        grad_in[at, :] = norm_back(
            tokens[at, :].astype(f32), input_gain[...], incoming
        ).astype(bf16)
        return carry

    lax.fori_loop(0, rows // chunk, in_chunk, 0)

    for copy in total_copies:
        copy.wait()
    sums = jnp.concatenate([sums_all[index].astype(f32) for index in range(ctx_size)], axis=1)
    offset = tp * slice_width - start
    share = pltpu.roll(sums[:, :width], lax.rem(width - offset, width), 1)[:, :slice_width]
    ups = sums[:, width : width + query_width]
    down_out_rows[...] = share[: 3 * rank]
    out_up_out[...] = share[3 * rank :]
    query_up_out[...] = ups[:rank]
    key_up_out[...] = ups[rank : 2 * rank, :head]
    value_up_out[...] = ups[rank : 2 * rank, head : 2 * head]
    out_down_out[...] = ups[2 * rank : 3 * rank]

    for hop in range(1, hops + 1):

        @pl.when(ctx + hop < ctx_size)
        def _(hop=hop):
            code_copy(hop).wait_send()

    for target, sent in (
        (1, even | (ctx >= 2)),
        (2, has_up),
        (3, (even & (ctx >= 2)) | (odd & (ctx >= 4))),
        (4, has_up & (ctx >= 2)),
    ):

        @pl.when(sent)
        def _(target=target):
            pair_copy(0, target, partner).wait_send()

    for place in range(4):

        @pl.when(sends[place])
        def _(place=place):
            back_copy(1, place, partner).wait_send()


def on_device(
    tokens,
    output_gradient,
    document_index,
    real_token_count,
    input_norm_gain,
    query_norm_gain,
    key_norm_gain,
    output_norm_gain,
    query_projection,
    key_projection,
    value_projection,
    output_projection,
    adapter_down_maps,
    adapter_query_up,
    adapter_key_up,
    adapter_value_up,
    adapter_output_down,
    adapter_output_up,
):
    rows, model = tokens.shape
    block = document_index.shape[0]
    head = key_projection.shape[1]
    query_width = query_projection.shape[1]
    rank = adapter_key_up.shape[0]
    ctx_size = lax.axis_size("ctx")
    tp_size = lax.axis_size("tp")
    reach = WINDOW // block
    hops = min(reach, ctx_size - 1)
    peers = max(tp_size - 1, 1)
    slice_width, width = window_of(model, tp_size)
    piece_width = -(-(width + query_width) // (LANES * ctx_size)) * LANES

    order = (0, 9, 10, 8, 12, 11, 1)
    arguments = (
        tokens,
        output_gradient,
        document_index.reshape(1, block),
        real_token_count,
        input_norm_gain,
        query_norm_gain.reshape(1, head),
        key_norm_gain.reshape(1, head),
        output_norm_gain,
        query_projection,
        key_projection,
        value_projection,
        output_projection,
        adapter_down_maps.T,
        adapter_query_up,
        adapter_key_up,
        adapter_value_up,
        adapter_output_down.T,
        adapter_output_up,
    )

    def kernel(*refs):
        inputs, results = list(refs[:18]), refs[18:26]
        buffers, sems, scratch = refs[26 : 26 + len(order)], refs[26 + len(order)], refs[27 + len(order) :]
        staged = {}
        for slot, place in enumerate(order):
            staged[place] = pltpu.make_async_copy(inputs[place], buffers[slot], sems.at[slot])
            staged[place].start()
            inputs[place] = buffers[slot]
        layer_kernel((ctx_size, tp_size, reach, hops), staged, *inputs, *results, *scratch)

    def copy_results(*refs):
        for place in range(8):
            refs[8 + place][...] = refs[place][...]

    whole = pl.BlockSpec(memory_space=pltpu.VMEM)
    in_specs = [whole] * 18
    in_specs[3] = pl.BlockSpec(memory_space=pltpu.SMEM)
    for place in order:
        in_specs[place] = pl.BlockSpec(memory_space=pl.ANY)
    out_shape = (
        jax.ShapeDtypeStruct((rows, model), bf16),
        jax.ShapeDtypeStruct((rows, model), bf16),
        jax.ShapeDtypeStruct((3 * rank, slice_width), f32),
        jax.ShapeDtypeStruct((rank, query_width), f32),
        jax.ShapeDtypeStruct((rank, head), f32),
        jax.ShapeDtypeStruct((rank, head), f32),
        jax.ShapeDtypeStruct((rank, query_width), f32),
        jax.ShapeDtypeStruct((rank, slice_width), f32),
    )
    results = pl.pallas_call(
        kernel,
        out_shape=out_shape,
        in_specs=in_specs,
        out_specs=(whole,) * 8,
        scratch_shapes=[
            *[pltpu.VMEM(arguments[place].shape, arguments[place].dtype) for place in order],
            pltpu.SemaphoreType.DMA((len(order),)),
            pltpu.VMEM((1, model), f32),
            pltpu.VMEM((1, model), f32),
            pltpu.VMEM((block, model), bf16),
            pltpu.VMEM((hops + 1, 8, block), jnp.int32),
            pltpu.VMEM((hops + 1, block, 2 * head), bf16),
            pltpu.VMEM((hops + 1, block, query_width // head * block), bf16),
            pltpu.VMEM((block, query_width), bf16),
            pltpu.VMEM((peers, rows, model), bf16),
            pltpu.VMEM((peers, rows, model), bf16),
            pltpu.VMEM((peers, rows, LANES), bf16),
            pltpu.VMEM((peers, rows, LANES), bf16),
            pltpu.VMEM((rows, model), f32),
            pltpu.VMEM((block, model), bf16),
            pltpu.VMEM((block, 2 * LANES), bf16),
            pltpu.VMEM((hops, block, 2 * head), bf16),
            pltpu.VMEM((hops, block, 2 * head), bf16),
            pltpu.VMEM((block, query_width), f32),
            pltpu.VMEM((block, head), f32),
            pltpu.VMEM((block, query_width + 2 * head), bf16),
            pltpu.VMEM((block, LANES), f32),
            pltpu.VMEM((block, LANES), bf16),
            pltpu.VMEM((peers, block, LANES), bf16),
            pltpu.VMEM((peers, rows, model), bf16),
            pltpu.VMEM((peers, rows, model), bf16),
            pltpu.VMEM((rows, model), f32),
            pltpu.VMEM((ctx_size, 4 * rank, piece_width), bf16),
            pltpu.VMEM((ctx_size - 1, 4 * rank, piece_width), bf16),
            pltpu.VMEM((ctx_size, 4 * rank, piece_width), bf16),
            pltpu.SemaphoreType.DMA((2, peers)),
            pltpu.SemaphoreType.DMA((2, hops)),
            pltpu.SemaphoreType.DMA((2, hops)),
            pltpu.SemaphoreType.DMA((2, peers)),
            pltpu.SemaphoreType.DMA((2, peers)),
            pltpu.SemaphoreType.DMA((2, peers)),
            pltpu.SemaphoreType.DMA((2, peers)),
            pltpu.SemaphoreType.DMA((2, hops)),
            pltpu.SemaphoreType.DMA((2, peers)),
            pltpu.SemaphoreType.DMA((2, peers)),
            pltpu.SemaphoreType.DMA((2, ctx_size - 1)),
            pltpu.SemaphoreType.DMA((2, ctx_size - 1)),
        ],
        compiler_params=pltpu.CompilerParams(
            collective_id=0, has_side_effects=True, vmem_limit_bytes=56 * 1024 * 1024
        ),
    )(*arguments)
    layer_out, grad_in, down, query, key, value, out_down, out_up = pl.pallas_call(
        copy_results,
        out_shape=out_shape,
        in_specs=[whole] * 8,
        out_specs=(whole,) * 8,
    )(*results)
    return layer_out, grad_in, down.T, query, key, value, out_down.T, out_up


def solution(mesh):
    in_specs = (
        P(("groups", "ctx", "tp"), None),
        P(("groups", "ctx", "tp"), None),
        P(("groups", "ctx")),
        P(("groups", "ctx")),
        P(),
        P(),
        P(),
        P(),
        P(None, "tp"),
        P(None, "tp"),
        P(None, "tp"),
        P("tp", None),
        P(),
        P(None, "tp"),
        P(None, "tp"),
        P(None, "tp"),
        P("tp", None),
        P(),
    )
    out_specs = (
        P(("groups", "ctx", "tp"), None),
        P(("groups", "ctx", "tp"), None),
        P(("groups", "tp"), None),
        P("groups", "tp"),
        P("groups", "tp"),
        P("groups", "tp"),
        P(("groups", "tp"), None),
        P("groups", "tp"),
    )
    return jax.shard_map(
        on_device, mesh=mesh, in_specs=in_specs, out_specs=out_specs, check_vma=False
    )
```

```python
import jax
import jax.numpy as jnp
from jax import lax
from jax.experimental import pallas as pl
from jax.experimental.pallas import tpu as pltpu
from jax.sharding import PartitionSpec as P

WINDOW = 1024
LANES = 128
NORM_ROWS = 32

epsilon = 1e-06
adapter_scale = 2.0
score_scale = 168.0 ** (-0.5)

bf16 = jnp.bfloat16
f32 = jnp.float32


def norm_rows(source, gain_vec):
    inverse = lax.rsqrt(jnp.mean(source * source, axis=-1, keepdims=True) + epsilon)
    return source * inverse * gain_vec


def norm_back(source, gain_vec, incoming):
    inverse = lax.rsqrt(jnp.mean(source * source, axis=-1, keepdims=True) + epsilon)
    scaled = source * inverse
    upward = incoming * gain_vec
    return inverse * (upward - scaled * jnp.mean(upward * scaled, axis=-1, keepdims=True))


def matrix_product(first_op, second_op):
    return jnp.dot(first_op, second_op, preferred_element_type=f32)


def multiply_by_transpose(first_op, second_op):
    return lax.dot_general(
        first_op, second_op, (((1,), (1,)), ((), ())), preferred_element_type=f32
    )


def window_of(model_width, tp_size):
    slice_width = model_width // tp_size
    if slice_width % LANES == 0:
        return slice_width, slice_width
    width = min(-(-(slice_width + LANES - 1) // LANES) * LANES, model_width)
    if tp_size == 2:
        width = -(-slice_width // LANES) * LANES
    return slice_width, width


def window_start(tp_index, slice_width, width, model_width):
    return jnp.minimum(tp_index * slice_width // LANES * LANES, model_width - width)


def layer_kernel(
    shapes,
    staged,
    tokens,
    output_gradient,
    documents,
    token_count,
    input_gain_vec,
    query_gain,
    key_gain,
    output_gain_vec,
    query_w,
    key_w,
    value_w,
    output_w,
    down_w,
    query_up,
    key_up,
    value_up,
    out_down,
    out_up,
    layer_out,
    grad_in,
    down_out_rows,
    query_up_out,
    key_up_out,
    value_up_out,
    out_down_out,
    out_up_out,
    input_gain,
    output_gain,
    normed,
    codes,
    pairs,
    weights,
    attended,
    out_send,
    out_recv,
    mid_send,
    mid_recv,
    pre_norm,
    grad_full,
    small_full,
    pair_grads,
    pair_recv,
    query_pre,
    key_pre,
    pre_grads,
    mid_pad,
    mid_grads,
    mid_grads_recv,
    normed_send,
    normed_recv,
    grad_normed,
    sums_send,
    sums_recv,
    sums_all,
    gather_sems,
    code_sems,
    pair_sems,
    out_sems,
    mid_sems,
    grad_sems,
    small_sems,
    back_sems,
    mid_grad_sems,
    normed_sems,
    sum_sems,
    total_sems,
):
    ctx_size, tp_size, reach, hops = shapes
    rows, model = tokens.shape
    chunk = min(NORM_ROWS, rows)
    block = documents.shape[1]
    head = key_w.shape[1]
    heads = query_w.shape[1] // head
    rank = key_up.shape[0]
    ctx = lax.axis_index("ctx")
    tp = lax.axis_index("tp")

    def tp_at(step):
        return lax.rem(tp + step, tp_size)

    def ctx_at(step):
        return lax.rem(ctx + step, ctx_size)

    def remote(source, target, sems, slot, where):
        return pltpu.make_async_remote_copy(
            src_ref=source,
            dst_ref=target,
            send_sem=sems.at[0, slot],
            recv_sem=sems.at[1, slot],
            device_id=where,
            device_id_type=pl.DeviceIdType.MESH,
        )

    def rows_of(index):
        return pl.ds(pl.multiple_of(index * rows, rows), rows)

    mine = rows_of(tp)

    barrier = pltpu.get_barrier_semaphore()
    for step in range(1, tp_size):
        pl.semaphore_signal(
            barrier, inc=1, device_id={"tp": tp_at(step)}, device_id_type=pl.DeviceIdType.MESH
        )
    for step in range(1, ctx_size):
        pl.semaphore_signal(
            barrier, inc=1, device_id={"ctx": ctx_at(step)}, device_id_type=pl.DeviceIdType.MESH
        )

    input_gain[...] = input_gain_vec[...].reshape(1, model)
    output_gain[...] = output_gain_vec[...].reshape(1, model)

    def norm_chunk(index, carry):
        at = pl.ds(index * chunk if isinstance(index, int) else pl.multiple_of(index * chunk, chunk), chunk)
        to = pl.ds(pl.multiple_of(tp * rows + index * chunk, chunk), chunk)
        normed[to, :] = norm_rows(tokens[at, :].astype(f32), input_gain[...]).astype(bf16)
        return carry

    staged[0].wait()
    lax.fori_loop(0, rows // chunk, norm_chunk, 0)

    lane_pos = lax.broadcasted_iota(jnp.int32, (1, block), 1)
    valid_lane = (lane_pos < token_count[0]).astype(f32)
    valid_sub = (
        lax.broadcasted_iota(jnp.int32, (block, 1), 0) < token_count[0]
    ).astype(f32)
    own_codes = jnp.where(lane_pos < token_count[0], documents[...] + 1, 0)
    codes[0] = jnp.broadcast_to(own_codes, codes.shape[1:])
    for hop in range(1, hops + 1):

        @pl.when(ctx < hop)
        def _(hop=hop):
            codes[hop] = jnp.zeros(codes.shape[1:], codes.dtype)
            pairs[hop] = jnp.zeros(pairs.shape[1:], pairs.dtype)

    odd = lax.rem(ctx, 2) == 1
    even = jnp.logical_not(odd)
    has_up = ctx + 2 < ctx_size
    partner = {"ctx": ctx + 1 - 2 * lax.rem(ctx, 2)}
    above = {"ctx": ctx_at(2)}
    below = {"ctx": ctx_at(ctx_size - 2)}
    arrives = (
        (even & (ctx >= 2)) | (odd & (ctx >= 5)),
        has_up & (ctx >= 2),
        even | (ctx >= 3),
        has_up,
    )
    sends = (
        (even & (ctx >= 4)) | (odd & (ctx >= 3)),
        ctx >= 4,
        odd | (ctx >= 2),
        ctx >= 2,
    )
    for place in range(4):

        @pl.when(jnp.logical_not(arrives[place]))
        def _(place=place):
            pair_recv[place] = jnp.zeros(pair_recv.shape[1:], pair_recv.dtype)

    pl.semaphore_wait(barrier, tp_size - 1 + ctx_size - 1)

    gathers = []
    for step in range(1, tp_size):
        copy = remote(
            normed.at[mine], normed.at[mine], gather_sems, step - 1, {"tp": tp_at(step)}
        )
        copy.start()
        gathers.append(copy)

    def code_copy(hop):
        return remote(codes.at[0], codes.at[hop], code_sems, hop - 1, {"ctx": ctx_at(hop)})

    def pair_copy(source, target, where):
        return remote(pairs.at[source], pairs.at[target], pair_sems, target - 1, where)

    def back_copy(hop, place, where):
        return remote(pair_grads.at[hop - 1], pair_recv.at[place], back_sems, place, where)

    pair_arrives = {1: odd | (ctx >= 2), 2: ctx >= 2, 3: ctx >= 3, 4: ctx >= 4}
    pair_arrives[3] = (odd & (ctx >= 3)) | (even & (ctx >= 4))

    for hop in range(1, hops + 1):

        @pl.when(ctx + hop < ctx_size)
        def _(hop=hop):
            code_copy(hop).start()

    for copy in gathers:
        copy.wait()

    for place in (9, 10, 8, 12):
        staged[place].wait()
    inputs = normed[...]
    middles = multiply_by_transpose(inputs, down_w[...]).astype(bf16)
    mid_pad[...] = jnp.zeros(mid_pad.shape, f32)
    mid_pad[:, : 3 * rank] = middles.astype(f32)

    def projected(weight, up, place):
        return matrix_product(inputs, weight[...]) + adapter_scale * matrix_product(
            middles[:, place * rank : (place + 1) * rank], up[...]
        )

    key_pre[...] = projected(key_w, key_up, 1)
    pairs[0, :, :head] = norm_rows(key_pre[...], key_gain[...]).astype(bf16)
    pairs[0, :, head:] = projected(value_w, value_up, 2).astype(bf16)

    @pl.when(has_up)
    def _():
        pair_copy(0, 2, above).start()

    @pl.when(even)
    def _():
        pair_copy(0, 1, partner).start()

    query_pre[...] = projected(query_w, query_up, 0)
    query_list = [
        norm_rows(query_pre[:, h * head : (h + 1) * head], query_gain[...]) for h in range(heads)
    ]
    query_rows = jnp.concatenate(query_list, axis=0).astype(bf16)
    query_cols = jnp.concatenate([q.T for q in query_list], axis=1).astype(bf16)

    sub = lax.broadcasted_iota(jnp.int32, (block, block), 0)
    lane = lax.broadcasted_iota(jnp.int32, (block, block), 1)
    wanted = (documents[...] + 1).astype(f32)
    totals = jnp.zeros((1, heads * block), f32)
    outputs = jnp.zeros((head, heads * block), f32)
    for hop in range(1, hops + 1):

        @pl.when(ctx >= hop)
        def _(hop=hop):
            code_copy(hop).wait_recv()

    def receive_pair(hop):
        @pl.when(pair_arrives[hop])
        def _():
            pair_copy(0, hop, partner).wait_recv()

    receive_pair(2)

    @pl.when(has_up & (ctx >= 2))
    def _():
        pair_copy(2, 4, above).start()

    @pl.when(even & (ctx >= 2))
    def _():
        pair_copy(2, 3, partner).start()

    @pl.when(odd & (ctx >= 2))
    def _():
        pair_copy(2, 1, partner).start()

    for hop in (0, 2, 1, 4, 3):
        if hop == 1:
            receive_pair(1)
            receive_pair(4)

            @pl.when(odd & (ctx >= 4))
            def _():
                pair_copy(4, 3, partner).start()

        if hop == 3:
            receive_pair(3)
        code_row = codes[hop][0:1, :].astype(f32)
        code_col = jnp.sum(jnp.where(sub == lane, code_row, 0.0), axis=1, keepdims=True)
        allowed = code_col == wanted
        if hop == 0:
            allowed = (sub == lane) | ((sub < lane) & allowed)
        if hop == reach:
            allowed = (sub > lane) & allowed
        allowed = allowed.astype(f32)
        allowed = jnp.concatenate([allowed] * heads, axis=1)
        scores = matrix_product(pairs[hop, :, :head], query_cols) * score_scale
        exps = jnp.where(allowed > 0.0, jnp.exp(scores), 0.0)
        totals = totals + jnp.sum(exps, axis=0, keepdims=True)
        exps = exps.astype(bf16)
        weights[hop] = exps
        values_cols = pairs[hop, :, head:].astype(f32).T.astype(bf16)
        outputs = outputs + matrix_product(values_cols, exps)
    inverse_totals = 1.0 / totals
    outputs = outputs * inverse_totals
    for h in range(heads):
        piece = outputs[:, h * block : (h + 1) * block] * valid_lane
        attended[:, h * head : (h + 1) * head] = piece.T.astype(bf16)

    staged[11].wait()
    mid_send[...] = jnp.zeros(mid_send.shape, bf16)
    out_copies = []
    for step in range(1, tp_size):
        theirs = attended[rows_of(tp_at(step)), :]
        mid_send[step - 1, :, :rank] = multiply_by_transpose(theirs, out_down[...]).astype(bf16)
        out_send[step - 1] = matrix_product(theirs, output_w[...]).astype(bf16)
        for source, target, sems in (
            (mid_send, mid_recv, mid_sems),
            (out_send, out_recv, out_sems),
        ):
            copy = remote(
                source.at[step - 1], target.at[step - 1], sems, step - 1, {"tp": tp_at(step)}
            )
            copy.start()
            out_copies.append(copy)
    own_rows = attended[mine, :]
    mid_sum = multiply_by_transpose(own_rows, out_down[...]).astype(bf16).astype(f32)
    pre_norm[...] = matrix_product(own_rows, output_w[...])
    for copy in out_copies:
        copy.wait()
    for step in range(1, tp_size):
        mid_sum = mid_sum + mid_recv[step - 1, :, :rank].astype(f32)
    mid_out = mid_sum.astype(bf16)
    pre_norm[...] += adapter_scale * matrix_product(mid_out, out_up[...])

    def out_chunk(index, carry):
        at = pl.ds(index * chunk if isinstance(index, int) else pl.multiple_of(index * chunk, chunk), chunk)
        to = pl.ds(pl.multiple_of(tp * rows + index * chunk, chunk), chunk)
        held = pre_norm[at, :]
        for step in range(1, tp_size):
            held = held + out_recv[step - 1, at, :].astype(f32)
        layer_out[at, :] = norm_rows(held, output_gain[...]).astype(bf16)
        grad_full[to, :] = norm_back(
            held, output_gain[...], output_gradient[at, :].astype(f32)
        ).astype(bf16)
        return carry

    staged[1].wait()

    grad_copies = []
    for index in range(rows // chunk):
        out_chunk(index, 0)
        part = pl.ds(pl.multiple_of(tp * rows + index * chunk, chunk), chunk)
        for step in range(1, tp_size):
            copy = remote(
                grad_full.at[part],
                grad_full.at[part],
                grad_sems,
                index * (tp_size - 1) + step - 1,
                {"tp": tp_at(step)},
            )
            copy.start()
            grad_copies.append(copy)
    grad_mid_out = adapter_scale * multiply_by_transpose(grad_full[mine, :], out_up[...])
    small_full[mine, :] = jnp.zeros((rows, 2 * LANES), bf16)
    small_full[mine, :rank] = grad_mid_out.astype(bf16)
    small_full[mine, LANES : LANES + rank] = mid_out
    for step in range(1, tp_size):
        copy = remote(
            small_full.at[mine], small_full.at[mine], small_sems, step - 1, {"tp": tp_at(step)}
        )
        copy.start()
        grad_copies.append(copy)
    for copy in grad_copies:
        copy.wait()

    grad_att = (
        multiply_by_transpose(grad_full[...], output_w[...])
        + matrix_product(small_full[:, :rank], out_down[...])
    ) * valid_sub
    grad_cols = jnp.concatenate(
        [grad_att[:, h * head : (h + 1) * head].T for h in range(heads)], axis=1
    ).astype(bf16)
    grad_float = grad_cols.astype(f32)
    inner = jnp.sum(grad_float * outputs, axis=0, keepdims=True)
    grad_rows = (grad_float * inverse_totals).T.astype(bf16)
    row_scale = inverse_totals * score_scale

    query_back = jnp.zeros((head, heads * block), f32)
    odd_share = odd.astype(f32)
    even_share = 1.0 - odd_share

    def receive_back(place):
        @pl.when(arrives[place])
        def _():
            back_copy(1, place, partner).wait_recv()

    def send_back(hop, place, where, sends):
        @pl.when(sends)
        def _():
            back_copy(hop, place, where).start()

    for hop in (3, 4, 1, 2, 0):
        keys = pairs[hop, :, :head]
        exps = weights[hop]
        probs_back = matrix_product(pairs[hop, :, head:], grad_cols)
        scores_back = (exps.astype(f32) * ((probs_back - inner) * row_scale)).astype(bf16)
        keys_back = matrix_product(scores_back, query_rows)
        values_back = matrix_product(exps, grad_rows)
        query_back = query_back + matrix_product(keys.astype(f32).T.astype(bf16), scores_back)
        pair_back = jnp.concatenate([keys_back, values_back], axis=1)
        if hop == 3:
            pair_grads[2] = pair_back.astype(bf16)
            send_back(3, 0, partner, sends[0])
        if hop == 4:
            receive_back(0)
            pair_back = pair_back + odd_share * pair_recv[0].astype(f32)
            pair_grads[3] = pair_back.astype(bf16)
            send_back(4, 1, below, sends[1])
        if hop == 1:
            pair_grads[0] = pair_back.astype(bf16)
            send_back(1, 2, partner, sends[2])
        if hop == 2:
            receive_back(2)
            receive_back(1)
            pair_back = pair_back + even_share * pair_recv[0].astype(f32)
            pair_back = pair_back + odd_share * pair_recv[2].astype(f32)
            pair_back = pair_back + pair_recv[1].astype(f32)
            pair_grads[1] = pair_back.astype(bf16)
            send_back(2, 3, below, sends[3])
        if hop == 0:
            own_pair = pair_back + even_share * pair_recv[2].astype(f32)
    query_width = heads * head
    for h in range(heads):
        at = slice(h * head, (h + 1) * head)
        pre_grads[:, at] = norm_back(
            query_pre[:, at], query_gain[...], query_back[:, h * block : (h + 1) * block].T
        ).astype(bf16)
    receive_back(3)
    own_pair = own_pair + pair_recv[3].astype(f32)
    own_keys, own_values = own_pair[:, :head], own_pair[:, head:]
    key_at = slice(query_width, query_width + head)
    value_at = slice(query_width + head, query_width + 2 * head)
    pre_grads[:, key_at] = norm_back(key_pre[...], key_gain[...], own_keys).astype(bf16)
    pre_grads[:, value_at] = own_values.astype(bf16)

    mid_grads[...] = jnp.zeros(mid_grads.shape, bf16)
    for place, (at, up) in enumerate(
        ((slice(0, query_width), query_up), (key_at, key_up), (value_at, value_up))
    ):
        mid_grads[:, place * rank : (place + 1) * rank] = (
            adapter_scale * multiply_by_transpose(pre_grads[:, at], up[...])
        ).astype(bf16)
    last_copies = []
    for step in range(1, tp_size):
        copy = remote(
            mid_grads, mid_grads_recv.at[step - 1], mid_grad_sems, step - 1, {"tp": tp_at(step)}
        )
        copy.start()
        last_copies.append(copy)

    def input_part(which):
        grads = pre_grads[which, :]
        return (
            multiply_by_transpose(grads[:, :query_width], query_w[...])
            + multiply_by_transpose(grads[:, key_at], key_w[...])
            + multiply_by_transpose(grads[:, value_at], value_w[...])
            + matrix_product(mid_grads[which, : 3 * rank], down_w[...])
        )

    slice_width, width = window_of(model, tp_size)
    start = window_start(tp, slice_width, width, model)
    window = pl.ds(pl.multiple_of(start, LANES), width)
    for copy in last_copies:
        copy.wait()
    mid_total = mid_grads[...].astype(f32)
    for step in range(1, tp_size):
        mid_total = mid_total + mid_grads_recv[step - 1].astype(f32)
    mid_total = mid_total.T[: 3 * rank].astype(bf16)
    middle_cols = mid_pad[...].T[: 3 * rank].astype(bf16)
    small_cols = small_full[...].astype(f32).T
    grad_mid_cols = small_cols[:rank].astype(bf16)
    mid_out_cols = small_cols[LANES : LANES + rank].astype(bf16)
    main_terms = jnp.concatenate(
        [
            matrix_product(mid_total, normed[:, window]),
            adapter_scale * matrix_product(mid_out_cols, grad_full[:, window]),
        ],
        axis=0,
    ).astype(bf16)
    up_terms = [
        adapter_scale * matrix_product(middle_cols[:rank], pre_grads[:, :query_width]),
        adapter_scale
        * jnp.concatenate(
            [
                matrix_product(middle_cols[rank : 2 * rank], pre_grads[:, key_at]),
                matrix_product(middle_cols[2 * rank :], pre_grads[:, value_at]),
            ],
            axis=1,
        ),
        matrix_product(grad_mid_cols, attended[...]),
        jnp.zeros((rank, query_width), f32),
    ]
    piece_width = sums_send.shape[2]
    padding = piece_width * ctx_size - width - query_width
    pieces = [main_terms, jnp.concatenate(up_terms, axis=0).astype(bf16)]
    if padding > 0:
        pieces.append(jnp.zeros((4 * rank, padding), bf16))
    every_term = jnp.concatenate(pieces, axis=1)
    for index in range(ctx_size):
        sums_send[index] = every_term[:, index * piece_width : (index + 1) * piece_width]
    sum_copies = []
    for step in range(1, ctx_size):
        copy = remote(
            sums_send.at[ctx_at(step)],
            sums_recv.at[step - 1],
            sum_sems,
            step - 1,
            {"ctx": ctx_at(step)},
        )
        copy.start()
        sum_copies.append(copy)

    normed_copies = []
    for step in range(1, tp_size):
        normed_send[step - 1] = input_part(rows_of(tp_at(step))).astype(bf16)
        copy = remote(
            normed_send.at[step - 1],
            normed_recv.at[step - 1],
            normed_sems,
            step - 1,
            {"tp": tp_at(step)},
        )
        copy.start()
        normed_copies.append(copy)

    grad_normed[...] = input_part(mine)
    for copy in sum_copies:
        copy.wait()
    total = sums_send[ctx].astype(f32)
    for step in range(1, ctx_size):
        total = total + sums_recv[step - 1].astype(f32)
    sums_all[ctx] = total.astype(bf16)
    total_copies = []
    for step in range(1, ctx_size):
        copy = remote(
            sums_all.at[ctx], sums_all.at[ctx], total_sems, step - 1, {"ctx": ctx_at(step)}
        )
        copy.start()
        total_copies.append(copy)

    for copy in normed_copies:
        copy.wait()

    def in_chunk(index, carry):
        at = pl.ds(index * chunk if isinstance(index, int) else pl.multiple_of(index * chunk, chunk), chunk)
        incoming = grad_normed[at, :]
        for step in range(1, tp_size):
            incoming = incoming + normed_recv[step - 1, at, :].astype(f32)
        grad_in[at, :] = norm_back(
            tokens[at, :].astype(f32), input_gain[...], incoming
        ).astype(bf16)
        return carry

    lax.fori_loop(0, rows // chunk, in_chunk, 0)

    for copy in total_copies:
        copy.wait()
    sums = jnp.concatenate([sums_all[index].astype(f32) for index in range(ctx_size)], axis=1)
    offset = tp * slice_width - start
    share = pltpu.roll(sums[:, :width], lax.rem(width - offset, width), 1)[:, :slice_width]
    ups = sums[:, width : width + query_width]
    down_out_rows[...] = share[: 3 * rank]
    out_up_out[...] = share[3 * rank :]
    query_up_out[...] = ups[:rank]
    key_up_out[...] = ups[rank : 2 * rank, :head]
    value_up_out[...] = ups[rank : 2 * rank, head : 2 * head]
    out_down_out[...] = ups[2 * rank : 3 * rank]

    for hop in range(1, hops + 1):

        @pl.when(ctx + hop < ctx_size)
        def _(hop=hop):
            code_copy(hop).wait_send()

    for target, sent in (
        (1, even | (ctx >= 2)),
        (2, has_up),
        (3, (even & (ctx >= 2)) | (odd & (ctx >= 4))),
        (4, has_up & (ctx >= 2)),
    ):

        @pl.when(sent)
        def _(target=target):
            pair_copy(0, target, partner).wait_send()

    for place in range(4):

        @pl.when(sends[place])
        def _(place=place):
            back_copy(1, place, partner).wait_send()


def on_device(
    tokens,
    output_gradient,
    document_index,
    real_token_count,
    input_norm_gain,
    query_norm_gain,
    key_norm_gain,
    output_norm_gain,
    query_projection,
    key_projection,
    value_projection,
    output_projection,
    adapter_down_maps,
    adapter_query_up,
    adapter_key_up,
    adapter_value_up,
    adapter_output_down,
    adapter_output_up,
):
    rows, model = tokens.shape
    block = document_index.shape[0]
    head = key_projection.shape[1]
    query_width = query_projection.shape[1]
    rank = adapter_key_up.shape[0]
    ctx_size = lax.axis_size("ctx")
    tp_size = lax.axis_size("tp")
    reach = WINDOW // block
    hops = min(reach, ctx_size - 1)
    peers = max(tp_size - 1, 1)
    slice_width, width = window_of(model, tp_size)
    piece_width = -(-(width + query_width) // (LANES * ctx_size)) * LANES

    order = (0, 9, 10, 8, 12, 11, 1)
    arguments = (
        tokens,
        output_gradient,
        document_index.reshape(1, block),
        real_token_count,
        input_norm_gain,
        query_norm_gain.reshape(1, head),
        key_norm_gain.reshape(1, head),
        output_norm_gain,
        query_projection,
        key_projection,
        value_projection,
        output_projection,
        adapter_down_maps.T,
        adapter_query_up,
        adapter_key_up,
        adapter_value_up,
        adapter_output_down.T,
        adapter_output_up,
    )

    def kernel(*refs):
        inputs, results = list(refs[:18]), refs[18:26]
        buffers, sems, scratch = refs[26 : 26 + len(order)], refs[26 + len(order)], refs[27 + len(order) :]
        staged = {}
        for slot, place in enumerate(order):
            staged[place] = pltpu.make_async_copy(inputs[place], buffers[slot], sems.at[slot])
            staged[place].start()
            inputs[place] = buffers[slot]
        layer_kernel((ctx_size, tp_size, reach, hops), staged, *inputs, *results, *scratch)

    def copy_results(*refs):
        for place in range(8):
            refs[8 + place][...] = refs[place][...]

    whole = pl.BlockSpec(memory_space=pltpu.VMEM)
    in_specs = [whole] * 18
    in_specs[3] = pl.BlockSpec(memory_space=pltpu.SMEM)
    for place in order:
        in_specs[place] = pl.BlockSpec(memory_space=pl.ANY)
    out_shape = (
        jax.ShapeDtypeStruct((rows, model), bf16),
        jax.ShapeDtypeStruct((rows, model), bf16),
        jax.ShapeDtypeStruct((3 * rank, slice_width), f32),
        jax.ShapeDtypeStruct((rank, query_width), f32),
        jax.ShapeDtypeStruct((rank, head), f32),
        jax.ShapeDtypeStruct((rank, head), f32),
        jax.ShapeDtypeStruct((rank, query_width), f32),
        jax.ShapeDtypeStruct((rank, slice_width), f32),
    )
    results = pl.pallas_call(
        kernel,
        out_shape=out_shape,
        in_specs=in_specs,
        out_specs=(whole,) * 8,
        scratch_shapes=[
            *[pltpu.VMEM(arguments[place].shape, arguments[place].dtype) for place in order],
            pltpu.SemaphoreType.DMA((len(order),)),
            pltpu.VMEM((1, model), f32),
            pltpu.VMEM((1, model), f32),
            pltpu.VMEM((block, model), bf16),
            pltpu.VMEM((hops + 1, 8, block), jnp.int32),
            pltpu.VMEM((hops + 1, block, 2 * head), bf16),
            pltpu.VMEM((hops + 1, block, query_width // head * block), bf16),
            pltpu.VMEM((block, query_width), bf16),
            pltpu.VMEM((peers, rows, model), bf16),
            pltpu.VMEM((peers, rows, model), bf16),
            pltpu.VMEM((peers, rows, LANES), bf16),
            pltpu.VMEM((peers, rows, LANES), bf16),
            pltpu.VMEM((rows, model), f32),
            pltpu.VMEM((block, model), bf16),
            pltpu.VMEM((block, 2 * LANES), bf16),
            pltpu.VMEM((hops, block, 2 * head), bf16),
            pltpu.VMEM((hops, block, 2 * head), bf16),
            pltpu.VMEM((block, query_width), f32),
            pltpu.VMEM((block, head), f32),
            pltpu.VMEM((block, query_width + 2 * head), bf16),
            pltpu.VMEM((block, LANES), f32),
            pltpu.VMEM((block, LANES), bf16),
            pltpu.VMEM((peers, block, LANES), bf16),
            pltpu.VMEM((peers, rows, model), bf16),
            pltpu.VMEM((peers, rows, model), bf16),
            pltpu.VMEM((rows, model), f32),
            pltpu.VMEM((ctx_size, 4 * rank, piece_width), bf16),
            pltpu.VMEM((ctx_size - 1, 4 * rank, piece_width), bf16),
            pltpu.VMEM((ctx_size, 4 * rank, piece_width), bf16),
            pltpu.SemaphoreType.DMA((2, peers)),
            pltpu.SemaphoreType.DMA((2, hops)),
            pltpu.SemaphoreType.DMA((2, hops)),
            pltpu.SemaphoreType.DMA((2, peers)),
            pltpu.SemaphoreType.DMA((2, peers)),
            pltpu.SemaphoreType.DMA((2, peers * (rows // min(NORM_ROWS, rows)))),
            pltpu.SemaphoreType.DMA((2, peers)),
            pltpu.SemaphoreType.DMA((2, hops)),
            pltpu.SemaphoreType.DMA((2, peers)),
            pltpu.SemaphoreType.DMA((2, peers)),
            pltpu.SemaphoreType.DMA((2, ctx_size - 1)),
            pltpu.SemaphoreType.DMA((2, ctx_size - 1)),
        ],
        compiler_params=pltpu.CompilerParams(
            collective_id=0, has_side_effects=True, vmem_limit_bytes=56 * 1024 * 1024
        ),
    )(*arguments)
    layer_out, grad_in, down, query, key, value, out_down, out_up = pl.pallas_call(
        copy_results,
        out_shape=out_shape,
        in_specs=[whole] * 8,
        out_specs=(whole,) * 8,
    )(*results)
    return layer_out, grad_in, down.T, query, key, value, out_down.T, out_up


def solution(mesh):
    in_specs = (
        P(("groups", "ctx", "tp"), None),
        P(("groups", "ctx", "tp"), None),
        P(("groups", "ctx")),
        P(("groups", "ctx")),
        P(),
        P(),
        P(),
        P(),
        P(None, "tp"),
        P(None, "tp"),
        P(None, "tp"),
        P("tp", None),
        P(),
        P(None, "tp"),
        P(None, "tp"),
        P(None, "tp"),
        P("tp", None),
        P(),
    )
    out_specs = (
        P(("groups", "ctx", "tp"), None),
        P(("groups", "ctx", "tp"), None),
        P(("groups", "tp"), None),
        P("groups", "tp"),
        P("groups", "tp"),
        P("groups", "tp"),
        P(("groups", "tp"), None),
        P("groups", "tp"),
    )
    return jax.shard_map(
        on_device, mesh=mesh, in_specs=in_specs, out_specs=out_specs, check_vma=False
    )
```
